256 devices in a mesh: seq: 16 (over x_hi, z), tensor: 16 (over x_lo, y, core).
Axes of the slice: x: 4 (x_hi: 2, x_lo: 2; x = x_hi * 2 + x_lo), y: 4, z: 8, core: 2. Of those that a mesh axis runs over, the one named last changes fastest.
Arguments:
- attn_heads: bfloat16 [8192, 8192], P('seq', 'tensor'), may hold values from -6 to 6
- out_weight: bfloat16 [8192, 8192], P('tensor'), may hold values from -0.0625 to 0.0625
- residual: bfloat16 [8192, 8192], P('seq', 'tensor'), may hold values from -40 to 40
- norm_gain: bfloat16 [8192], P('tensor'), may hold values from 0.25 to 1.75
- proj: bfloat16 [8192, 4096], P('tensor', 'seq'), may hold values from -0.0625 to 0.0625
- student_hidden: bfloat16 [8192, 4096], P(('seq', 'tensor')), may hold values from -6 to 6
Outputs:
- mismatch: float32 [8192, 4096], P(('seq', 'tensor'))
- grad_proj: float32 [4096, 8192], P('seq', 'tensor')
The draws below stay inside these ranges and needn't reach their ends.
All inputs are finite; a program needn't handle non-finite values.
Results may differ from the reference program's by a relative error of at most 0.015.
Values may be sent and summed in bfloat16 or wider, within the bound.
A program may use at most 128 MiB of HBM per device.

```python
import math
import jax
import jax.numpy as jnp
from jax import lax

TD = 8192
SD = 4096
TOKENS = 8192
N_TENSOR = 16


def draw_residual(key, part):
    key = jax.random.fold_in(key, 7)
    key_base, key_rows = jax.random.split(key)
    column = jnp.arange(TD, dtype=jnp.float32) / (TD - 1)
    col_scale = jnp.power(10.0, column) / 3.16
    row_scale = jnp.power(10.0, jax.random.uniform(key_rows, (TOKENS, 1), jnp.float32)) / 3.16
    base = jnp.clip(jax.random.normal(key_base, (TOKENS, TD), jnp.float32), -4.0, 4.0)
    return (base * row_scale * col_scale[None, :]).astype(jnp.bfloat16)


def block_scale(key, extent, shards, smallest, high):
    def one(dim, parts):
        draws = jax.random.uniform(jax.random.fold_in(jax.random.fold_in(key, 6), dim), (parts,), jnp.float32, smallest / len(shards), high / len(shards))
        return jnp.repeat(jnp.exp(draws), extent[dim] // parts).reshape((-1,) + (1,) * (len(extent) - dim - 1))

    factor_of = one(*shards[0])
    for cut in shards[1:]:
        factor_of = factor_of * one(*cut)
    return factor_of


def gaussian(rng, extent, scale, reach, pieces=(), kind=jnp.bfloat16):
    array = scale * jax.random.normal(rng, extent, jnp.float32)
    if pieces:
        array = array * block_scale(rng, extent, pieces, -0.22, 0.18)
    return jnp.clip(array, -reach, reach).astype(kind)


def setup_inputs(seed: int = 0) -> dict:
    key_of = jax.random.split(jax.random.key(seed), 7)
    return {
        "attn_heads": gaussian(key_of[0], (TOKENS, TD), 1.0, 6.0, ((0, 16), (1, 16))),
        "out_weight": gaussian(key_of[1], (TD, TD), TD ** -0.5, 0.0625, ((0, 16),)),
        "residual": draw_residual(jax.random.fold_in(key_of[6], 71), 0),
        "norm_gain": jnp.clip(1.0 + 0.15 * jax.random.normal(key_of[3], (TD,), jnp.float32), 0.25, 1.75).astype(jnp.bfloat16),
        "proj": gaussian(key_of[4], (TD, SD), TD ** -0.5, 0.0625, ((0, 16), (1, 16))),
        "student_hidden": gaussian(key_of[5], (TOKENS, SD), 1.0, 6.0, ((0, 256),)),
    }


def blockwise(left, right, width):
    rows = left.shape[0]
    cols = right.shape[1]

    def step(index, total):
        start = (index * width).astype(jnp.int32)
        block_left = lax.dynamic_slice_in_dim(left, start, width, 1)
        block_right = lax.dynamic_slice_in_dim(right, start, width, 0)
        product = jnp.dot(block_left, block_right, preferred_element_type=jnp.float32)
        rounded = lax.optimization_barrier(product.astype(jnp.bfloat16))
        return total + rounded.astype(jnp.float32)
    return lax.fori_loop(0, N_TENSOR, step, jnp.zeros((rows, cols), jnp.float32))

def reference(attn_heads, out_weight, residual, norm_gain, proj, student_hidden):
    width = TD // N_TENSOR
    teacher_hidden = residual.astype(jnp.float32) + blockwise(attn_heads, out_weight, width)
    power = lax.optimization_barrier(jnp.mean(teacher_hidden * teacher_hidden, axis=1, keepdims=True))
    normed = (teacher_hidden * lax.rsqrt(power + 1e-05) * norm_gain.astype(jnp.float32)).astype(jnp.bfloat16)
    projected = jnp.dot(normed, proj, preferred_element_type=jnp.float32)
    mismatch = projected - student_hidden.astype(jnp.float32)
    mismatch_low = mismatch.astype(jnp.bfloat16)
    scale = 1.0 / math.sqrt(TOKENS)
    grad_proj = scale * jnp.dot(mismatch_low.T, normed, preferred_element_type=jnp.float32)
    return (mismatch, grad_proj)
```

```python
import math

import jax
import jax.numpy as jnp
from jax import lax
from jax.experimental import pallas as pl
from jax.experimental.pallas import tpu as pltpu
from jax.sharding import PartitionSpec as P

MESH = pl.DeviceIdType.MESH
F32 = jnp.float32
BF16 = jnp.bfloat16
PAIRS = 8
STAGES = 7


def dot(a, b, dims=((1,), (0,))):
    return lax.dot_general(a, b, (dims, ((), ())), preferred_element_type=F32)


def kernel(
    attn, weight, resid, gain, proj, student,
    mis_out, grad_out,
    attn_v, res_v, w_v, stu_v,
    a_send, a_own, a_crecv, a_xrecv, ya_half, ya_full, yb_half, yb_full, xb_recv,
    hg, pw, pw_recv, r_v,
    pj,
    t_send, t_own, t_crecv, xr0, yr0, yr1, xr1, m_all,
    g_send, ring, rx,
    sem_attn, sem_res, sem_stu, sem_w, sem_proj,
    ac_s, ac_r, ax_s, ax_r, ay_s, ay_r, by_s, by_r, bx_s, bx_r,
    pw_s, pw_r, cx_s, cx_r, cz_s, cz_r,
    d_s, d_r, f_s, f_r, fx_s, fx_r,
):
    s = lax.axis_index("seq")
    t = lax.axis_index("tensor")
    xh, z = s // 8, s % 8
    x, y, c = t // 8, (t // 2) % 4, t % 2

    def at(xh_, z_, x_, y_, c_):
        return (xh_ * 8 + z_, x_ * 8 + y_ * 2 + c_)

    sib = at(xh, z, x, y, 1 - c)
    xdev = at(xh, z, 1 - x, y, c)
    xhdev = at(1 - xh, z, x, y, c)
    zdev = (at(xh, (z + 1) % 8, x, y, c), at(xh, (z + 7) % 8, x, y, c))

    def ydev(o):
        return at(xh, z, x, (y + o) % 4, c)

    def remote(src, dst, ss, rs, dev):
        return pltpu.make_async_remote_copy(
            src_ref=src, dst_ref=dst, send_sem=ss, recv_sem=rs, device_id=dev, device_id_type=MESH
        )

    def tokens(i):
        return (i % 8) // 4 * 8 + (i % 4) * 2 + i // 8

    def load_rows(src, dst, sem):
        def one(i, carry):
            row = pl.multiple_of(tokens(i) * 32, 32)
            pltpu.make_async_copy(src.at[pl.ds(row, 32)], dst.at[i], sem).start()
            return carry

        lax.fori_loop(0, 16, one, 0)

    def block_of(j, xo, co):
        dy = 2 - j + (j // 2) * (3 - 2 * (j % 2))
        return xo * 8 + (y + dy) % 4 * 2 + co

    def load_w(j):
        def one(i, carry):
            b = block_of(j, (x + 1 + i % 2) % 2, (c + 1 + i // 2) % 2)
            col = pl.multiple_of(b * 512, 512)
            pltpu.make_async_copy(weight.at[:, pl.ds(col, 512)], w_v.at[b], sem_w.at[b]).start()
            return carry

        lax.fori_loop(0, 4, one, 0)

    pltpu.make_async_copy(proj, pj.at[s], sem_proj).start()
    load_rows(attn, attn_v, sem_attn)
    for j in range(4):
        load_w(j)
    load_rows(resid, res_v, sem_res)
    pltpu.make_async_copy(student, stu_v, sem_stu).start()

    ring[:, 0, 0, 128:256] = jnp.zeros((2, 128, 512), BF16)
    ring[:, 1, 0, 0:128] = jnp.zeros((2, 128, 512), BF16)

    barrier = pltpu.get_barrier_semaphore()

    def greet(i, carry):
        pl.semaphore_signal(barrier, inc=1, device_id=(s, (t + i) % 16), device_id_type=MESH)
        return carry

    lax.fori_loop(1, 16, greet, 0)
    for dev in (xhdev,) + zdev:
        pl.semaphore_signal(barrier, inc=1, device_id=dev, device_id_type=MESH)
    pl.semaphore_wait(barrier, 18)

    def cz(line, dr, j):
        sign = 1 - 2 * dr
        xx = xh if line == 1 else 1 - xh
        b = xx * 8 + (z - sign * (j - 1) + 8) % 8
        ref = pj.at[b]
        if j == 4:
            ref = pj.at[b, pl.ds(256 * dr, 256)]
        return remote(ref, ref, cz_s.at[line, dr, j - 1], cz_r.at[line, dr, j - 1], zdev[dr])

    def cx():
        return remote(pj.at[s], pj.at[s], cx_s, cx_r, xhdev)

    def forward(line, j):
        for dr in range(2):
            if j > 1:
                cz(line, dr, j - 1).wait_recv()
            cz(line, dr, j).start()

    pltpu.make_async_copy(proj, pj.at[s], sem_proj).wait()
    cx().start()
    forward(1, 1)

    def ac(j, xo):
        return remote(a_send.at[j, xo], a_crecv.at[j, xo], ac_s.at[j, xo], ac_r.at[j, xo], sib)

    def ax(j):
        return remote(a_own.at[j, 1 - x, pl.ds(0, 256)], a_xrecv.at[j], ax_s.at[j], ax_r.at[j], xdev)

    def a_half(dr):
        return remote(
            a_own.at[0, x, pl.ds(128 * dr, 128)], ya_half.at[dr], ay_s.at[0, dr], ay_r.at[0, dr], ydev(1 + 2 * dr)
        )

    def a_full(dr):
        return remote(
            a_own.at[1 + dr, x, pl.ds(0, 256)], ya_full.at[dr], ay_s.at[1, dr], ay_r.at[1, dr], ydev(1 + 2 * dr)
        )

    def b_half(dr):
        return remote(
            a_own.at[0, :, pl.ds(256 + 128 * dr, 128)], yb_half.at[dr], by_s.at[0, dr], by_r.at[0, dr],
            ydev(1 + 2 * dr),
        )

    def b_full(dr):
        return remote(
            a_own.at[1 + dr, :, pl.ds(256, 256)], yb_full.at[dr], by_s.at[1, dr], by_r.at[1, dr], ydev(1 + 2 * dr)
        )

    def bx():
        return remote(a_own.at[3, 1 - x, pl.ds(256, 256)], xb_recv, bx_s, bx_r, xdev)

    def product(j, xo, co, out):
        b = block_of(j, xo, co)
        col = pl.multiple_of(b * 512, 512)
        pltpu.make_async_copy(weight.at[:, pl.ds(col, 512)], w_v.at[b], sem_w.at[b]).wait()
        out[j, xo] = dot(attn_v[...].reshape(512, 512), w_v[b]).astype(BF16)

    def multiply(j):
        def other(i, carry):
            xo = (x + 1 + i) % 2
            product(j, xo, 1 - c, a_send)
            ac(j, xo).start()
            return carry

        def own(i, carry):
            product(j, (x + 1 + i) % 2, c, a_own)
            return carry

        lax.fori_loop(0, 2, other, 0)
        lax.fori_loop(0, 2, own, 0)

    def combine(j):
        def one(i, carry):
            xo = (x + 1 + i) % 2
            ac(j, xo).wait_recv()
            a_own[j, xo] = (a_own[j, xo].astype(F32) + a_crecv[j, xo].astype(F32)).astype(BF16)

            @pl.when(i == 0)
            def _():
                ax(j).start()

            return carry

        lax.fori_loop(0, 2, one, 0)

        @pl.when(j == 0)
        def _():
            b_half(0).start()
            b_half(1).start()

    pltpu.make_async_copy(attn, attn, sem_attn).wait()

    def teacher(i, carry):
        @pl.when(i < 4)
        def _():
            multiply(i)

        @pl.when(i >= 1)
        def _():
            combine(i - 1)

        return carry

    lax.fori_loop(0, 5, teacher, 0)
    cx().wait_recv()
    forward(0, 1)
    forward(1, 2)

    def add_a(j):
        ax(j).wait_recv()
        a_own[j, x, 0:256] = (a_own[j, x, 0:256].astype(F32) + a_xrecv[j].astype(F32)).astype(BF16)

    add_a(0)
    for dr in range(2):
        a_half(dr).start()
    for dr in range(2):
        rows = slice(256 + 128 * dr, 384 + 128 * dr)
        b_half(dr).wait_recv()
        a_own[1 + dr, :, rows] = (a_own[1 + dr, :, rows].astype(F32) + yb_half[dr].astype(F32)).astype(BF16)
        b_full(dr).start()
    forward(0, 2)
    forward(1, 3)
    for dr in range(2):
        rows = slice(128 * dr, 128 * dr + 128)
        add_a(1 + dr)
        a_half(dr).wait_recv()
        a_own[1 + dr, x, rows] = (a_own[1 + dr, x, rows].astype(F32) + ya_half[dr].astype(F32)).astype(BF16)
        a_full(dr).start()
    b_full(0).wait_recv()
    b_full(1).wait_recv()
    a_own[3, :, 256:512] = (
        a_own[3, :, 256:512].astype(F32) + yb_full[0].astype(F32) + yb_full[1].astype(F32)
    ).astype(BF16)
    bx().start()
    forward(0, 3)
    add_a(3)
    a_full(0).wait_recv()
    a_full(1).wait_recv()
    pltpu.make_async_copy(resid, resid, sem_res).wait()

    def finish(co, total):
        hidden = total + res_v[pl.ds(8 * co, 8)].astype(F32).reshape(256, 512)
        hg[co] = (hidden * gain[...].astype(F32)).astype(BF16)
        sq = hidden * hidden
        sq = sq[:, 0:128] + sq[:, 128:256] + sq[:, 256:384] + sq[:, 384:512]
        pw[pl.ds(8 * co, 8)] = sq.reshape(8, 32, 128)

    finish(0, a_own[3, x, 0:256].astype(F32) + ya_full[0].astype(F32) + ya_full[1].astype(F32))
    forward(1, 4)
    bx().wait_recv()
    finish(1, a_own[3, x, 256:512].astype(F32) + xb_recv[...].astype(F32))

    def power(i):
        to = (t + i) % 16
        return remote(
            pw.at[to % 2 * 8 + to // 8 * 4 + to // 2 % 4], pw_recv.at[i], pw_s.at[i], pw_r.at[i], (s, to)
        )

    def send_power(i, carry):
        power(i).start()
        return carry

    lax.fori_loop(1, 16, send_power, 0)
    forward(0, 4)

    def root():
        def one(i, total):
            power(i).wait_recv()
            power(i).wait_send()
            return total + pw_recv[i]

        total = lax.fori_loop(1, 16, one, pw[c * 8 + x * 4 + y])
        mean = jnp.sum(total, axis=1, keepdims=True) * (1.0 / 8192)
        r_v[...] = jnp.broadcast_to(lax.rsqrt(mean + 1e-05), (32, 256))

    pltpu.make_async_copy(student, stu_v, sem_stu).wait()
    for line in range(2):
        for dr in range(2):
            cz(line, dr, 4).wait_recv()

    def block(g, m):
        mid = 1 - (g + 1) // 8 - (7 - g) // 7
        line = (1 - mid) * m + mid * ((g + 1) % 2)
        xx = (xh + 1 + line) % 2
        off = (1 - 2 * m) * (4 - (g + 1) // 2)
        return xx * 8 + (z + off + 8) % 8

    def ds_(k, i):
        return d_s.at[k, i], d_r.at[k, i]

    def dc(k):
        return remote(t_send.at[k], t_crecv.at[k], *ds_(k, 0), sib)

    def dx(g, m):
        k = 2 * g + m
        if m == 0:
            return remote(t_own.at[k, 1 - x], xr0.at[g], *ds_(k, 1), xdev)
        return remote(t_own.at[k, 1 - x, y], xr1.at[g], *ds_(k, 1), xdev)

    def dy(g, m, o):
        k = 2 * g + m
        if m == 0:
            return remote(t_own.at[k, x, (y + o) % 4], yr0.at[g, o - 1], *ds_(k, 1 + o), ydev(o))
        return remote(t_own.at[k, :, (y + o) % 4], yr1.at[g, o - 1], *ds_(k, 1 + o), ydev(o))

    def ex(g, m):
        k = 2 * g + m
        ref = m_all.at[k, c, x] if m == 0 else m_all.at[k, c, x, y]
        return remote(ref, ref, *ds_(k, 5), xdev)

    def ey(g, m, o):
        k = 2 * g + m
        ref = m_all.at[k, c, x, y] if m == 0 else m_all.at[k, c, :, y]
        return remote(ref, ref, *ds_(k, 5 + o), ydev(o))

    def ec(k):
        return remote(m_all.at[k, c], m_all.at[k, c], *ds_(k, 9), sib)

    def fz(line, dr, j, src):
        dst = ring.at[line, dr, j]
        return remote(src, dst, f_s.at[line, dr, j], f_r.at[line, dr, j], zdev[dr])

    def fz_half(line, dr):
        rows = pl.ds(128 * dr, 128)
        return remote(
            g_send.at[line, rows], ring.at[line, dr, 0, rows], f_s.at[line, dr, 0], f_r.at[line, dr, 0], zdev[dr]
        )

    def fx():
        return remote(g_send.at[14], rx, fx_s, fx_r, xhdev)

    def stage0(g, m):
        k = 2 * g + m
        b = block(g, m)
        t_send[k] = dot(hg[1 - c], pj[b]).astype(BF16).reshape(2, 4, 32, 256)
        dc(k).start()
        t_own[k] = dot(hg[c], pj[b]).astype(BF16).reshape(2, 4, 32, 256)

    def stage1(g, m):
        k = 2 * g + m
        dc(k).wait_recv()
        t_own[k] = (t_own[k].astype(F32) + t_crecv[k].astype(F32)).astype(BF16)
        if m == 0:
            dx(g, m).start()
        else:
            for o in (2, 1, 3):
                dy(g, m, o).start()

    def stage2(g, m):
        k = 2 * g + m
        dc(k).wait_send()
        if m == 0:
            dx(g, m).wait_recv()
            t_own[k, x] = (t_own[k, x].astype(F32) + xr0[g].astype(F32)).astype(BF16)
            for o in (2, 1, 3):
                dy(g, m, o).start()
        else:
            total = t_own[k, :, y].astype(F32)
            for o in (1, 2, 3):
                dy(g, m, o).wait_recv()
                total = total + yr1[g, o - 1].astype(F32)
            t_own[k, :, y] = total.astype(BF16)
            dx(g, m).start()

    def stage3(g, m):
        k = 2 * g + m
        if m == 0:
            total = t_own[k, x, y].astype(F32)
            for o in (1, 2, 3):
                dy(g, m, o).wait_recv()
                total = total + yr0[g, o - 1].astype(F32)
        else:
            dx(g, m).wait_recv()
            total = t_own[k, x, y].astype(F32) + xr1[g].astype(F32)
        cols = pl.ds(pl.multiple_of(block(g, m) * 256, 256), 256)
        mismatch = total * r_v[...] - stu_v[:, cols].astype(F32)
        mis_out[:, cols] = mismatch
        m_all[k, c, x, y] = (mismatch * r_v[...]).astype(BF16)
        if m == 0:
            for o in (2, 1, 3):
                ey(g, m, o).start()
        else:
            ex(g, m).start()
        dx(g, m).wait_send()
        for o in (1, 2, 3):
            dy(g, m, o).wait_send()

    def stage4(g, m):
        if m == 0:
            for o in (1, 2, 3):
                ey(g, m, o).wait_recv()
            ex(g, m).start()
        else:
            ex(g, m).wait_recv()
            for o in (2, 1, 3):
                ey(g, m, o).start()

    def stage5(g, m):
        if m == 0:
            ex(g, m).wait_recv()
        else:
            for o in (1, 2, 3):
                ey(g, m, o).wait_recv()
        ec(2 * g + m).start()
        ex(g, m).wait_send()
        for o in (1, 2, 3):
            ey(g, m, o).wait_send()

    def stage6(g, m):
        k = 2 * g + m
        ec(k).wait_recv()
        part = dot(m_all[k].reshape(512, 256), hg[...].reshape(512, 512), ((0,), (0,)))

        @pl.when(g == 0)
        def _():
            g_send[m] = part.astype(BF16)
            fz_half(m, 0).start()
            fz_half(m, 1).start()

        @pl.when((g > 0) & (g < 7))
        def _():
            line, j = (g + 1) % 2, (g + 1) // 2 - 1

            @pl.when(j == 0)
            def _():
                fz_half(line, m).wait_recv()

            @pl.when(j > 0)
            def _():
                fz(line, m, j, g_send.at[k]).wait_recv()

            g_send[k] = (part + ring[line, m, j].astype(F32)).astype(BF16)
            fz(line, m, j + 1, g_send.at[k]).start()

        @pl.when(g == 7)
        def _():
            fz(m, 0, 3, g_send.at[k]).wait_recv()
            fz(m, 1, 3, g_send.at[k]).wait_recv()
            total = part + ring[m, 0, 3].astype(F32) + ring[m, 1, 3].astype(F32)
            if m == 0:
                g_send[k] = total.astype(BF16)
                fx().start()
            else:
                fx().wait_recv()
                grad_out[...] = (total + rx[...].astype(F32)) * (1.0 / math.sqrt(8192))

        ec(k).wait_send()

    stages = (stage0, stage1, stage2, stage3, stage4, stage5, stage6)

    def student_step(i, carry):
        for n in reversed(range(STAGES)):
            @pl.when((i >= n) & (i < PAIRS + n))
            def _():
                stages[n](i - n, 0)
                stages[n](i - n, 1)

        @pl.when(i == 2)
        def _():
            root()

        return carry

    lax.fori_loop(0, PAIRS + STAGES - 1, student_step, 0)

    cx().wait_send()
    for line in range(2):
        for dr in range(2):
            for j in range(1, 5):
                cz(line, dr, j).wait_send()
            fz_half(line, dr).wait_send()
            for j in range(1, 4):
                fz(line, dr, j, g_send.at[0]).wait_send()
    for j in range(4):
        for xo in range(2):
            ac(j, xo).wait_send()
        ax(j).wait_send()
    for dr in range(2):
        a_half(dr).wait_send()
        a_full(dr).wait_send()
        b_half(dr).wait_send()
        b_full(dr).wait_send()
    bx().wait_send()
    fx().wait_send()


def shards(attn_heads, out_weight, residual, norm_gain, proj, student_hidden):
    hbm = pl.BlockSpec(memory_space=pl.ANY)
    vmem = pl.BlockSpec(memory_space=pltpu.VMEM)
    buf = lambda *shape: pltpu.VMEM(shape, BF16)
    dma = lambda *shape: pltpu.SemaphoreType.DMA(shape)
    return pl.pallas_call(
        kernel,
        name="distill",
        out_shape=(
            jax.ShapeDtypeStruct((32, 4096), F32),
            jax.ShapeDtypeStruct((256, 512), F32),
        ),
        in_specs=[hbm, hbm, hbm, vmem, hbm, hbm],
        out_specs=(vmem, vmem),
        scratch_shapes=[
            buf(16, 32, 512), buf(16, 32, 512), buf(16, 512, 512), buf(32, 4096),
            buf(4, 2, 512, 512), buf(4, 2, 512, 512), buf(4, 2, 512, 512), buf(4, 256, 512),
            buf(2, 128, 512), buf(2, 256, 512), buf(2, 2, 128, 512), buf(2, 2, 256, 512), buf(256, 512),
            buf(2, 256, 512), pltpu.VMEM((16, 32, 128), F32), pltpu.VMEM((16, 32, 128), F32),
            pltpu.VMEM((32, 256), F32),
            buf(16, 512, 256),
            buf(16, 2, 4, 32, 256), buf(16, 2, 4, 32, 256), buf(16, 2, 4, 32, 256),
            buf(8, 4, 32, 256), buf(8, 3, 32, 256), buf(8, 3, 2, 32, 256), buf(8, 32, 256),
            buf(16, 2, 2, 4, 32, 256),
            buf(16, 256, 512), buf(2, 2, 4, 256, 512), buf(256, 512),
            dma(), dma(), dma(), dma(16), dma(),
            dma(4, 2), dma(4, 2), dma(4), dma(4), dma(2, 2), dma(2, 2), dma(2, 2), dma(2, 2), dma(), dma(),
            dma(16), dma(16), dma(), dma(), dma(2, 2, 4), dma(2, 2, 4),
            dma(16, 10), dma(16, 10), dma(2, 2, 4), dma(2, 2, 4), dma(), dma(),
        ],
        compiler_params=pltpu.CompilerParams(
            collective_id=0, has_side_effects=True, vmem_limit_bytes=62 * 2**20
        ),
    )(attn_heads, out_weight, residual, norm_gain.reshape(1, 512), proj, student_hidden)


def solution(mesh):
    return jax.shard_map(
        shards,
        mesh=mesh,
        in_specs=(
            P("seq", "tensor"),
            P("tensor", None),
            P("seq", "tensor"),
            P("tensor"),
            P("tensor", "seq"),
            P(("seq", "tensor"), None),
        ),
        out_specs=(P(("seq", "tensor"), None), P("seq", "tensor")),
        check_vma=False,
    )
```

```python
import math

import jax
import jax.numpy as jnp
from jax import lax
from jax.experimental import pallas as pl
from jax.experimental.pallas import tpu as pltpu
from jax.sharding import PartitionSpec as P

MESH = pl.DeviceIdType.MESH
F32 = jnp.float32
BF16 = jnp.bfloat16
BLOCKS = 8
STEPS = (0, 1, 3, 5, 7, 9, 10, 11)
ROWS_A = 160
HALF_A, HALF_B = ROWS_A // 2, (512 - ROWS_A) // 2


def dot(a, b, dims=((1,), (0,))):
    return lax.dot_general(a, b, (dims, ((), ())), preferred_element_type=F32)


def kernel(
    attn, weight, resid, gain, proj, student,
    mis_out, grad_out,
    attn_v, res_v, w_v, stu_v,
    a_send, a_own, a_crecv, a_xrecv, ya_half, ya_full, yb_half, yb_full, xb_recv,
    hg, pw, pw_recv, r_v,
    pj,
    t_send, t_own, t_crecv, xr0, yr0, yr1, xr1, m_all,
    g_acc, g_send, ring, rx, mis_v, grad_v,
    sem_attn, sem_res, sem_stu, sem_w, sem_proj, sem_mis, sem_grad,
    ac_s, ac_r, ax_s, ax_r, ay_s, ay_r, by_s, by_r, bx_s, bx_r,
    pw_s, pw_r, cx_s, cx_r, cz_s, cz_r,
    d_s, d_r, f_s, f_r, fx_s, fx_r,
):
    s = lax.axis_index("seq")
    t = lax.axis_index("tensor")
    xh, z = s // 8, s % 8
    x, y, c = t // 8, (t // 2) % 4, t % 2

    def at(xh_, z_, x_, y_, c_):
        return (xh_ * 8 + z_, x_ * 8 + y_ * 2 + c_)

    sib = at(xh, z, x, y, 1 - c)
    xdev = at(xh, z, 1 - x, y, c)
    xhdev = at(1 - xh, z, x, y, c)
    zdev = (at(xh, (z + 1) % 8, x, y, c), at(xh, (z + 7) % 8, x, y, c))

    def ydev(o):
        return at(xh, z, x, (y + o) % 4, c)

    def remote(src, dst, ss, rs, dev):
        return pltpu.make_async_remote_copy(
            src_ref=src, dst_ref=dst, send_sem=ss, recv_sem=rs, device_id=dev, device_id_type=MESH
        )

    barrier = pltpu.get_barrier_semaphore()

    def greet(i, carry):
        pl.semaphore_signal(barrier, inc=1, device_id=(s, (t + i) % 16), device_id_type=MESH)
        return carry

    lax.fori_loop(1, 16, greet, 0)
    for dev in (xhdev,) + zdev:
        pl.semaphore_signal(barrier, inc=1, device_id=dev, device_id_type=MESH)

    def tokens(i):
        return (i % 8) // 4 * 8 + (i % 4) * 2 + i // 8

    def load_rows(src, dst, sem):
        def one(i, carry):
            row = pl.multiple_of(tokens(i) * 32, 32)
            pltpu.make_async_copy(src.at[pl.ds(row, 32)], dst.at[i], sem).start()
            return carry

        lax.fori_loop(0, 16, one, 0)

    def block_of(j, xo, co):
        dy = 2 - j + (j // 2) * (3 - 2 * (j % 2))
        return xo * 8 + (y + dy) % 4 * 2 + co

    def load_w(j):
        def one(i, carry):
            b = block_of(j, (x + 1 + i % 2) % 2, (c + 1 + i // 2) % 2)
            col = pl.multiple_of(b * 512, 512)
            pltpu.make_async_copy(weight.at[:, pl.ds(col, 512)], w_v.at[b], sem_w.at[b]).start()
            return carry

        lax.fori_loop(0, 4, one, 0)

    pltpu.make_async_copy(proj, pj.at[s], sem_proj).start()
    load_rows(attn, attn_v, sem_attn)
    for j in range(4):
        load_w(j)
    load_rows(resid, res_v, sem_res)
    pltpu.make_async_copy(student, stu_v, sem_stu).start()

    ring[:, 0, 0, 128:256] = jnp.zeros((2, 128, 512), BF16)
    ring[:, 1, 0, 0:128] = jnp.zeros((2, 128, 512), BF16)

    pl.semaphore_wait(barrier, 18)

    def cz(line, dr, j, p):
        sign = 1 - 2 * dr
        xx = xh if line == 1 else 1 - xh
        b = xx * 8 + (z - sign * (j - 1) + 8) % 8
        if j == 4:
            ref = pj.at[b, pl.ds(256 * dr + 128 * p, 128)]
        else:
            ref = pj.at[b, pl.ds(256 * p, 256)]
        return remote(ref, ref, cz_s.at[line, dr, j - 1, p], cz_r.at[line, dr, j - 1, p], zdev[dr])

    def cx():
        return remote(pj.at[s], pj.at[s], cx_s, cx_r, xhdev)

    def arrived(line, j, p):
        for dr in range(2):
            if j == 3:
                if p == 0:
                    cz(line, dr, j, 0).wait_recv()
                    cz(line, dr, j, 1).wait_recv()
            else:
                cz(line, dr, j, p).wait_recv()

    def forward(line, j, p):
        if j > 1:
            arrived(line, j - 1, p)
        for dr in range(2):
            cz(line, dr, j, p).start()

    pltpu.make_async_copy(proj, pj.at[s], sem_proj).wait()
    cx().start()
    forward(1, 1, 0)
    forward(1, 1, 1)

    def ac(j, xo):
        return remote(a_send.at[j, xo], a_crecv.at[j, xo], ac_s.at[j, xo], ac_r.at[j, xo], sib)

    def ax(j):
        return remote(a_own.at[j, 1 - x, pl.ds(0, ROWS_A)], a_xrecv.at[j], ax_s.at[j], ax_r.at[j], xdev)

    def a_half(dr):
        return remote(
            a_own.at[0, x, pl.ds(HALF_A * dr, HALF_A)], ya_half.at[dr], ay_s.at[0, dr], ay_r.at[0, dr], ydev(1 + 2 * dr)
        )

    def a_full(dr):
        return remote(
            a_own.at[1 + dr, x, pl.ds(0, ROWS_A)], ya_full.at[dr], ay_s.at[1, dr], ay_r.at[1, dr], ydev(1 + 2 * dr)
        )

    def b_half(dr, xo):
        return remote(
            a_own.at[0, xo, pl.ds(ROWS_A + HALF_B * dr, HALF_B)], yb_half.at[dr, xo], by_s.at[0, dr, xo], by_r.at[0, dr, xo],
            ydev(1 + 2 * dr),
        )

    def b_full(dr, xo):
        return remote(
            a_own.at[1 + dr, xo, pl.ds(ROWS_A, 2 * HALF_B)], yb_full.at[dr, xo], by_s.at[1, dr, xo], by_r.at[1, dr, xo],
            ydev(1 + 2 * dr),
        )

    def bx():
        return remote(a_own.at[3, 1 - x, pl.ds(ROWS_A, 2 * HALF_B)], xb_recv, bx_s, bx_r, xdev)

    def product(j, xo, co, out):
        b = block_of(j, xo, co)
        col = pl.multiple_of(b * 512, 512)
        pltpu.make_async_copy(weight.at[:, pl.ds(col, 512)], w_v.at[b], sem_w.at[b]).wait()
        out[j, xo] = dot(attn_v[...].reshape(512, 512), w_v[b]).astype(BF16)

    def unit(u):
        return u // 2, (x + 1 + u % 2) % 2

    def multiply(u):
        j, xo = unit(u)
        product(j, xo, 1 - c, a_send)
        ac(j, xo).start()
        product(j, xo, c, a_own)

    def combine(u):
        j, xo = unit(u)
        ac(j, xo).wait_recv()
        a_own[j, xo] = (a_own[j, xo].astype(F32) + a_crecv[j, xo].astype(F32)).astype(BF16)

        @pl.when(u % 2 == 0)
        def _():
            ax(j).start()

        @pl.when(u < 2)
        def _():
            b_half(0, xo).start()
            b_half(1, xo).start()

    def send_b(dr, xo):
        rows = slice(ROWS_A + HALF_B * dr, ROWS_A + HALF_B * dr + HALF_B)
        b_half(dr, xo).wait_recv()
        a_own[1 + dr, xo, rows] = (a_own[1 + dr, xo, rows].astype(F32) + yb_half[dr, xo].astype(F32)).astype(BF16)
        b_full(dr, xo).start()

    def add_a(j):
        ax(j).wait_recv()
        a_own[j, x, 0:ROWS_A] = (a_own[j, x, 0:ROWS_A].astype(F32) + a_xrecv[j].astype(F32)).astype(BF16)

    pltpu.make_async_copy(attn, attn, sem_attn).wait()

    def teacher(u, carry):
        @pl.when(u < 8)
        def _():
            multiply(u)

        @pl.when(u >= 1)
        def _():
            combine(u - 1)

        @pl.when(u == 4)
        def _():
            forward(1, 2, 0)

        @pl.when(u == 6)
        def _():
            forward(1, 2, 1)

        @pl.when(u == 7)
        def _():
            send_b(0, 1 - x)
            send_b(1, 1 - x)

        return carry

    lax.fori_loop(0, 9, teacher, 0)

    def send_a(dr):
        rows = slice(HALF_A * dr, HALF_A * dr + HALF_A)
        add_a(1 + dr)
        a_half(dr).wait_recv()
        a_own[1 + dr, x, rows] = (a_own[1 + dr, x, rows].astype(F32) + ya_half[dr].astype(F32)).astype(BF16)
        a_full(dr).start()

    def sum_b(xo):
        b_full(0, xo).wait_recv()
        b_full(1, xo).wait_recv()
        a_own[3, xo, ROWS_A:512] = (
            a_own[3, xo, ROWS_A:512].astype(F32) + yb_full[0, xo].astype(F32) + yb_full[1, xo].astype(F32)
        ).astype(BF16)

    add_a(0)
    for dr in range(2):
        a_half(dr).start()
    for dr in range(2):
        send_b(dr, x)
    cx().wait_recv()
    forward(0, 1, 0)
    forward(0, 1, 1)
    forward(0, 2, 0)
    send_a(0)
    forward(0, 2, 1)
    send_a(1)
    sum_b(1 - x)
    bx().start()
    forward(0, 3, 0)
    forward(0, 3, 1)
    add_a(3)
    sum_b(x)
    forward(0, 4, 0)
    forward(0, 4, 1)
    forward(1, 3, 0)
    forward(1, 3, 1)
    a_full(0).wait_recv()
    a_full(1).wait_recv()
    pltpu.make_async_copy(resid, resid, sem_res).wait()

    def finish(lo, hi, total):
        hidden = total + res_v[lo // 32 : hi // 32].astype(F32).reshape(hi - lo, 512)
        hg[lo:hi] = (hidden * gain[...].astype(F32)).astype(BF16)
        sq = hidden * hidden
        sq = sq[:, 0:128] + sq[:, 128:256] + sq[:, 256:384] + sq[:, 384:512]
        pw[lo // 32 : hi // 32] = sq.reshape((hi - lo) // 32, 32, 128)

    finish(0, ROWS_A, a_own[3, x, 0:ROWS_A].astype(F32) + ya_full[0].astype(F32) + ya_full[1].astype(F32))
    bx().wait_recv()
    finish(ROWS_A, 512, a_own[3, x, ROWS_A:512].astype(F32) + xb_recv[...].astype(F32))

    def power(i):
        to = (t + i) % 16
        return remote(
            pw.at[to % 2 * 8 + to // 8 * 4 + to // 2 % 4], pw_recv.at[i], pw_s.at[i], pw_r.at[i], (s, to)
        )

    def send_power(i, carry):
        power(i).start()
        return carry

    lax.fori_loop(1, 16, send_power, 0)

    def root():
        def one(i, total):
            power(i).wait_recv()
            power(i).wait_send()
            return total + pw_recv[i]

        total = lax.fori_loop(1, 16, one, pw[c * 8 + x * 4 + y])
        mean = jnp.sum(total, axis=1, keepdims=True) * (1.0 / 8192)
        r_v[...] = jnp.broadcast_to(lax.rsqrt(mean + 1e-05), (32, 256))

    pltpu.make_async_copy(student, stu_v, sem_stu).wait()
    arrived(0, 4, 0)
    arrived(0, 4, 1)

    def block(q, m):
        line = (q + 3 + 2 * m) // 8
        off = (1 - 2 * m) * (4 - q - m + 4 * line)
        return (xh + 1 + line) % 2 * 8 + (z + off + 8) % 8

    def ds_(k, i):
        return d_s.at[k, i], d_r.at[k, i]

    def dc(k):
        return remote(t_send.at[k], t_crecv.at[k], *ds_(k, 0), sib)

    def dx(g, m):
        k = 2 * g + m
        if m == 0:
            return remote(t_own.at[k, 1 - x], xr0.at[g], *ds_(k, 1), xdev)
        return remote(t_own.at[k, 1 - x, y], xr1.at[g], *ds_(k, 1), xdev)

    def dy(g, m, o):
        k = 2 * g + m
        if m == 0:
            return remote(t_own.at[k, x, (y + o) % 4], yr0.at[g, o - 1], *ds_(k, 1 + o), ydev(o))
        return remote(t_own.at[k, :, (y + o) % 4], yr1.at[g, o - 1], *ds_(k, 1 + o), ydev(o))

    def ex(g, m):
        k = 2 * g + m
        ref = m_all.at[k, c, x] if m == 0 else m_all.at[k, c, x, y]
        return remote(ref, ref, *ds_(k, 5), xdev)

    def ey(g, m, o):
        k = 2 * g + m
        ref = m_all.at[k, c, x, y] if m == 0 else m_all.at[k, c, :, y]
        return remote(ref, ref, *ds_(k, 5 + o), ydev(o))

    def ec(k):
        return remote(m_all.at[k, c], m_all.at[k, c], *ds_(k, 9), sib)

    def fz(line, dr, j, p, k):
        cols = pl.ds(256 * p, 256)
        return remote(
            g_send.at[k, :, cols], ring.at[line, dr, j, :, cols], f_s.at[line, dr, j, p], f_r.at[line, dr, j, p],
            zdev[dr],
        )

    def fz_half(line, dr, p, k):
        rows, cols = pl.ds(128 * dr, 128), pl.ds(256 * p, 256)
        return remote(
            g_send.at[k, rows, cols], ring.at[line, dr, 0, rows, cols], f_s.at[line, dr, 0, p],
            f_r.at[line, dr, 0, p], zdev[dr],
        )

    def fx(p):
        cols = pl.ds(256 * p, 256)
        return remote(g_send.at[8, :, cols], rx.at[:, cols], fx_s.at[p], fx_r.at[p], xhdev)

    def core_rows(co):
        return pl.ds(pl.multiple_of(co * 256, 256), 256)

    def stage0(g, m):
        k = 2 * g + m
        b = block(g, m)
        t_send[k] = dot(hg[core_rows(1 - c)], pj[b]).astype(BF16).reshape(2, 4, 32, 256)
        dc(k).start()
        t_own[k] = dot(hg[core_rows(c)], pj[b]).astype(BF16).reshape(2, 4, 32, 256)

    def stage1(g, m):
        k = 2 * g + m
        dc(k).wait_recv()
        t_own[k] = (t_own[k].astype(F32) + t_crecv[k].astype(F32)).astype(BF16)
        if m == 0:
            dx(g, m).start()
        else:
            for o in (2, 1, 3):
                dy(g, m, o).start()

    def stage2(g, m):
        k = 2 * g + m
        dc(k).wait_send()
        if m == 0:
            dx(g, m).wait_recv()
            t_own[k, x] = (t_own[k, x].astype(F32) + xr0[g].astype(F32)).astype(BF16)
            for o in (2, 1, 3):
                dy(g, m, o).start()
        else:
            total = t_own[k, :, y].astype(F32)
            for o in (1, 2, 3):
                dy(g, m, o).wait_recv()
                total = total + yr1[g, o - 1].astype(F32)
            t_own[k, :, y] = total.astype(BF16)
            dx(g, m).start()

    def stage3(g, m):
        k = 2 * g + m
        if m == 0:
            total = t_own[k, x, y].astype(F32)
            for o in (1, 2, 3):
                dy(g, m, o).wait_recv()
                total = total + yr0[g, o - 1].astype(F32)
        else:
            dx(g, m).wait_recv()
            total = t_own[k, x, y].astype(F32) + xr1[g].astype(F32)
        cols = pl.ds(pl.multiple_of(block(g, m) * 256, 256), 256)
        mismatch = total * r_v[...] - stu_v[:, cols].astype(F32)
        mis_v[:, cols] = mismatch
        m_all[k, c, x, y] = (mismatch * r_v[...]).astype(BF16)
        if m == 0:
            for o in (2, 1, 3):
                ey(g, m, o).start()
        else:
            ex(g, m).start()
        dx(g, m).wait_send()
        for o in (1, 2, 3):
            dy(g, m, o).wait_send()

    def stage4(g, m):
        if m == 0:
            for o in (1, 2, 3):
                ey(g, m, o).wait_recv()
            ex(g, m).start()
        else:
            ex(g, m).wait_recv()
            for o in (2, 1, 3):
                ey(g, m, o).start()

    def stage5(g, m):
        if m == 0:
            ex(g, m).wait_recv()
        else:
            for o in (1, 2, 3):
                ey(g, m, o).wait_recv()
        ec(2 * g + m).start()
        ex(g, m).wait_send()
        for o in (1, 2, 3):
            ey(g, m, o).wait_send()

    def put_grad(p):
        cols = pl.ds(256 * p, 256)
        return pltpu.make_async_copy(grad_v.at[:, cols], grad_out.at[:, cols], sem_grad.at[p])

    def put_mis():
        return pltpu.make_async_copy(mis_v, mis_out, sem_mis)

    def stage6(q, m):
        k = 2 * q + m
        ec(k).wait_recv()
        g_acc[m] = dot(m_all[k].reshape(512, 256), hg[...], ((0,), (0,)))
        ec(k).wait_send()
        reduce(q, m, 0)

    def stage7(q, m):
        reduce(q, m, 1)

    def reduce(q, m, p):
        k = 2 * q + m
        cols = slice(256 * p, 256 * p + 256)
        part = g_acc[m, :, cols]

        @pl.when(q == 3 * m)
        def _():
            g_send[k, :, cols] = part.astype(BF16)
            fz_half(m, 0, p, k).start()
            fz_half(m, 1, p, k).start()

        @pl.when(q == 4 + 3 * m)
        def _():
            for dr in range(2):
                fz(m, dr, 3, p, k).wait_recv()
            total = part + ring[m, 0, 3, :, cols].astype(F32) + ring[m, 1, 3, :, cols].astype(F32)
            if m == 0:
                g_send[k, :, cols] = total.astype(BF16)
                fx(p).start()
            else:
                fx(p).wait_recv()
                grad_v[:, cols] = (total + rx[:, cols].astype(F32)) * (1.0 / math.sqrt(8192))
                put_grad(p).start()

        @pl.when((q != 3 * m) & (q != 4 + 3 * m))
        def _():
            line = (q + 3 + 2 * m) // 8
            j = q + m - 1 - 4 * line

            @pl.when(j == 0)
            def _():
                fz_half(line, m, p, k).wait_recv()

            @pl.when(j > 0)
            def _():
                fz(line, m, j, p, k).wait_recv()

            g_send[k, :, cols] = (part + ring[line, m, j, :, cols].astype(F32)).astype(BF16)
            fz(line, m, j + 1, p, k).start()

    stages = (stage0, stage1, stage2, stage3, stage4, stage5, stage6, stage7)

    def student_steps(h, carry):
        for par in range(2):
            for n in reversed(range(len(stages))):
                m = (par - STEPS[n]) % 2
                q = h + (par - STEPS[n] - m) // 2
                pl.when((q >= 0) & (q < BLOCKS))(lambda: stages[n](q, m))

            if par == 0:

                @pl.when(h == 2)
                def _():
                    root()
                    forward(1, 4, 0)
                    forward(1, 4, 1)

                @pl.when(h == 3)
                def _():
                    arrived(1, 4, 0)
                    arrived(1, 4, 1)

                @pl.when(h == 11)
                def _():
                    put_mis().start()

        return carry

    lax.fori_loop(0, BLOCKS + (STEPS[-1] + 1) // 2, student_steps, 0)

    cx().wait_send()
    for line in range(2):
        for dr in range(2):
            for j in range(1, 5):
                cz(line, dr, j, 0).wait_send()
                cz(line, dr, j, 1).wait_send()
            for p in range(2):
                fz_half(line, dr, p, 0).wait_send()
                for j in range(1, 4):
                    fz(line, dr, j, p, 0).wait_send()
    for j in range(4):
        for xo in range(2):
            ac(j, xo).wait_send()
        ax(j).wait_send()
    for dr in range(2):
        a_half(dr).wait_send()
        a_full(dr).wait_send()
        for xo in range(2):
            b_half(dr, xo).wait_send()
            b_full(dr, xo).wait_send()
    bx().wait_send()
    fx(0).wait_send()
    fx(1).wait_send()
    put_mis().wait()
    put_grad(0).wait()
    put_grad(1).wait()


def shards(attn_heads, out_weight, residual, norm_gain, proj, student_hidden):
    hbm = pl.BlockSpec(memory_space=pl.ANY)
    vmem = pl.BlockSpec(memory_space=pltpu.VMEM)
    buf = lambda *shape: pltpu.VMEM(shape, BF16)
    dma = lambda *shape: pltpu.SemaphoreType.DMA(shape)
    return pl.pallas_call(
        kernel,
        name="distill",
        out_shape=(
            jax.ShapeDtypeStruct((32, 4096), F32),
            jax.ShapeDtypeStruct((256, 512), F32),
        ),
        in_specs=[hbm, hbm, hbm, vmem, hbm, hbm],
        out_specs=(hbm, hbm),
        scratch_shapes=[
            buf(16, 32, 512), buf(16, 32, 512), buf(16, 512, 512), buf(32, 4096),
            buf(4, 2, 512, 512), buf(4, 2, 512, 512), buf(4, 2, 512, 512), buf(4, ROWS_A, 512),
            buf(2, HALF_A, 512), buf(2, ROWS_A, 512), buf(2, 2, HALF_B, 512), buf(2, 2, 2 * HALF_B, 512),
            buf(2 * HALF_B, 512),
            buf(512, 512), pltpu.VMEM((16, 32, 128), F32), pltpu.VMEM((16, 32, 128), F32),
            pltpu.VMEM((32, 256), F32),
            buf(16, 512, 256),
            buf(16, 2, 4, 32, 256), buf(16, 2, 4, 32, 256), buf(16, 2, 4, 32, 256),
            buf(8, 4, 32, 256), buf(8, 3, 32, 256), buf(8, 3, 2, 32, 256), buf(8, 32, 256),
            buf(16, 2, 2, 4, 32, 256),
            pltpu.VMEM((2, 256, 512), F32), buf(16, 256, 512), buf(2, 2, 4, 256, 512), buf(256, 512),
            pltpu.VMEM((32, 4096), F32), pltpu.VMEM((256, 512), F32),
            dma(), dma(), dma(), dma(16), dma(), dma(), dma(2),
            dma(4, 2), dma(4, 2), dma(4), dma(4), dma(2, 2), dma(2, 2), dma(2, 2, 2), dma(2, 2, 2), dma(), dma(),
            dma(16), dma(16), dma(), dma(), dma(2, 2, 4, 2), dma(2, 2, 4, 2),
            dma(16, 10), dma(16, 10), dma(2, 2, 4, 2), dma(2, 2, 4, 2), dma(2), dma(2),
        ],
        compiler_params=pltpu.CompilerParams(
            collective_id=0, has_side_effects=True, vmem_limit_bytes=62 * 2**20
        ),
    )(attn_heads, out_weight, residual, norm_gain.reshape(1, 512), proj, student_hidden)


def solution(mesh):
    return jax.shard_map(
        shards,
        mesh=mesh,
        in_specs=(
            P("seq", "tensor"),
            P("tensor", None),
            P("seq", "tensor"),
            P("tensor"),
            P("tensor", "seq"),
            P(("seq", "tensor"), None),
        ),
        out_specs=(P(("seq", "tensor"), None), P("seq", "tensor")),
        check_vma=False,
    )
```

```python
import math

import jax
import jax.numpy as jnp
from jax import lax
from jax.experimental import pallas as pl
from jax.experimental.pallas import tpu as pltpu
from jax.sharding import PartitionSpec as P

MESH = pl.DeviceIdType.MESH
F32 = jnp.float32
BF16 = jnp.bfloat16
BLOCKS = 8
STEPS = (0, 1, 3, 5, 7, 9, 10, 11)
ROWS_A = 160
HALF_A, HALF_B = ROWS_A // 2, (512 - ROWS_A) // 2


def dot(a, b, dims=((1,), (0,))):
    return lax.dot_general(a, b, (dims, ((), ())), preferred_element_type=F32)


def kernel(
    attn, weight, resid, gain, proj, student,
    mis_out, grad_out,
    attn_v, res_v, w_v, stu_v,
    a_send, a_own, a_crecv, a_xrecv, ya_half, ya_full, yb_half, yb_full, xb_recv,
    hg, pw, pw_recv, r_v,
    pj,
    t_send, t_own, t_crecv, xr0, yr0, yr1, xr1, m_all,
    g_acc, g_send, ring, rx, mis_v, grad_v,
    sem_attn, sem_res, sem_stu, sem_w, sem_proj, sem_mis, sem_grad,
    ac_s, ac_r, ax_s, ax_r, ay_s, ay_r, by_s, by_r, bx_s, bx_r,
    pw_s, pw_r, cx_s, cx_r, cz_s, cz_r,
    d_s, d_r, f_s, f_r, fx_s, fx_r,
):
    s = lax.axis_index("seq")
    t = lax.axis_index("tensor")
    xh, z = s // 8, s % 8
    x, y, c = t // 8, (t // 2) % 4, t % 2

    def at(xh_, z_, x_, y_, c_):
        return (xh_ * 8 + z_, x_ * 8 + y_ * 2 + c_)

    sib = at(xh, z, x, y, 1 - c)
    xdev = at(xh, z, 1 - x, y, c)
    xhdev = at(1 - xh, z, x, y, c)
    zdev = (at(xh, (z + 1) % 8, x, y, c), at(xh, (z + 7) % 8, x, y, c))

    def ydev(o):
        return at(xh, z, x, (y + o) % 4, c)

    def remote(src, dst, ss, rs, dev):
        return pltpu.make_async_remote_copy(
            src_ref=src, dst_ref=dst, send_sem=ss, recv_sem=rs, device_id=dev, device_id_type=MESH
        )

    barrier = pltpu.get_barrier_semaphore()

    def greet(i, carry):
        pl.semaphore_signal(barrier, inc=1, device_id=(s, (t + i) % 16), device_id_type=MESH)
        return carry

    lax.fori_loop(1, 16, greet, 0)
    for dev in (xhdev,) + zdev:
        pl.semaphore_signal(barrier, inc=1, device_id=dev, device_id_type=MESH)

    def whole(ref, ss, rs):
        return remote(ref, ref, ss, rs, sib)

    def tokens(i):
        return (i % 8) // 4 * 8 + (i % 4) * 2 + i // 8

    def load_rows(src, dst, sem):
        def one(i, carry):
            row = pl.multiple_of(tokens(i) * 32, 32)
            pltpu.make_async_copy(src.at[pl.ds(row, 32)], dst.at[i], sem).start()
            return carry

        lax.fori_loop(0, 16, one, 0)

    def block_of(j, xo, co):
        dy = 2 - j + (j // 2) * (3 - 2 * (j % 2))
        return xo * 8 + (y + dy) % 4 * 2 + co

    def load_w(u):
        b = block_of(u // 2, (x + 1 + u % 2) % 2, 0) // 2
        col = pl.multiple_of(b * 1024, 1024)
        return pltpu.make_async_copy(weight.at[:, pl.ds(col, 1024)], w_v.at[u], sem_w.at[u])

    pltpu.make_async_copy(proj, pj.at[s], sem_proj).start()
    load_rows(attn, attn_v, sem_attn)
    for u in range(8):
        load_w(u).start()
    load_rows(resid, res_v, sem_res)
    pltpu.make_async_copy(student, stu_v, sem_stu).start()

    ring[:, 0, 0, 128:256] = jnp.zeros((2, 128, 512), BF16)
    ring[:, 1, 0, 0:128] = jnp.zeros((2, 128, 512), BF16)

    pl.semaphore_wait(barrier, 18)

    def cz(line, dr, j, p):
        sign = 1 - 2 * dr
        xx = xh if line == 1 else 1 - xh
        b = xx * 8 + (z - sign * (j - 1) + 8) % 8
        if j == 4:
            ref = pj.at[b, pl.ds(256 * dr + 128 * p, 128)]
        else:
            ref = pj.at[b, pl.ds(256 * p, 256)]
        return remote(ref, ref, cz_s, cz_r.at[line, dr, j - 1, p], zdev[dr])

    def cx():
        return remote(pj.at[s], pj.at[s], cx_s, cx_r, xhdev)

    def arrived(line, j, p):
        for dr in range(2):
            if j == 3:
                if p == 0:
                    cz(line, dr, j, 0).wait_recv()
                    cz(line, dr, j, 1).wait_recv()
            else:
                cz(line, dr, j, p).wait_recv()

    def forward(line, j, p):
        if j > 1:
            arrived(line, j - 1, p)
        for dr in range(2):
            cz(line, dr, j, p).start()

    pltpu.make_async_copy(proj, pj.at[s], sem_proj).wait()
    cx().start()
    forward(1, 1, 0)
    forward(1, 1, 1)

    def ac(j, xo):
        return remote(a_send.at[j, xo], a_crecv.at[j, xo], ac_s, ac_r.at[j, xo], sib)

    def ax(j):
        return remote(a_own.at[j, 1 - x, pl.ds(0, ROWS_A)], a_xrecv.at[j], ax_s, ax_r.at[j], xdev)

    def a_half(dr):
        return remote(
            a_own.at[0, x, pl.ds(HALF_A * dr, HALF_A)], ya_half.at[dr], ay_s.at[0], ay_r.at[0, dr], ydev(1 + 2 * dr)
        )

    def a_full(dr):
        return remote(
            a_own.at[1 + dr, x, pl.ds(0, ROWS_A)], ya_full.at[dr], ay_s.at[1], ay_r.at[1, dr], ydev(1 + 2 * dr)
        )

    def b_half(dr, xo):
        return remote(
            a_own.at[0, xo, pl.ds(ROWS_A + HALF_B * dr, HALF_B)], yb_half.at[dr, xo], by_s.at[0], by_r.at[0, dr, xo],
            ydev(1 + 2 * dr),
        )

    def b_full(dr, xo):
        return remote(
            a_own.at[1 + dr, xo, pl.ds(ROWS_A, 2 * HALF_B)], yb_full.at[dr, xo], by_s.at[1], by_r.at[1, dr, xo],
            ydev(1 + 2 * dr),
        )

    def bx():
        return remote(a_own.at[3, 1 - x, pl.ds(ROWS_A, 2 * HALF_B)], xb_recv, bx_s, bx_r, xdev)

    def product(u, co, out):
        j, xo = unit(u)
        cols = pl.ds(pl.multiple_of(co * 512, 512), 512)
        out[j, xo] = dot(attn_v[...].reshape(512, 512), w_v[u, :, cols]).astype(BF16)

    def unit(u):
        return u // 2, (x + 1 + u % 2) % 2

    def multiply(u):
        j, xo = unit(u)
        load_w(u).wait()
        product(u, 1 - c, a_send)
        ac(j, xo).start()
        product(u, c, a_own)

    def combine(u):
        j, xo = unit(u)
        ac(j, xo).wait_recv()
        a_own[j, xo] = (a_own[j, xo].astype(F32) + a_crecv[j, xo].astype(F32)).astype(BF16)

        @pl.when(u % 2 == 0)
        def _():
            ax(j).start()

        @pl.when(u < 2)
        def _():
            b_half(0, xo).start()
            b_half(1, xo).start()

    def send_b(dr, xo):
        rows = slice(ROWS_A + HALF_B * dr, ROWS_A + HALF_B * dr + HALF_B)
        b_half(dr, xo).wait_recv()
        a_own[1 + dr, xo, rows] = (a_own[1 + dr, xo, rows].astype(F32) + yb_half[dr, xo].astype(F32)).astype(BF16)
        b_full(dr, xo).start()

    def add_a(j):
        ax(j).wait_recv()
        a_own[j, x, 0:ROWS_A] = (a_own[j, x, 0:ROWS_A].astype(F32) + a_xrecv[j].astype(F32)).astype(BF16)

    pltpu.make_async_copy(attn, attn, sem_attn).wait()

    def teacher(u, carry):
        @pl.when(u < 8)
        def _():
            multiply(u)

        @pl.when(u >= 1)
        def _():
            combine(u - 1)

        @pl.when(u == 6)
        def _():
            forward(1, 2, 0)

        @pl.when(u == 7)
        def _():
            send_b(0, 1 - x)
            send_b(1, 1 - x)
            cx().wait_recv()
            forward(0, 1, 0)
            forward(0, 1, 1)

        return carry

    lax.fori_loop(0, 9, teacher, 0)

    def send_a(dr):
        rows = slice(HALF_A * dr, HALF_A * dr + HALF_A)
        add_a(1 + dr)
        a_half(dr).wait_recv()
        a_own[1 + dr, x, rows] = (a_own[1 + dr, x, rows].astype(F32) + ya_half[dr].astype(F32)).astype(BF16)
        a_full(dr).start()

    def sum_b(xo):
        b_full(0, xo).wait_recv()
        b_full(1, xo).wait_recv()
        a_own[3, xo, ROWS_A:512] = (
            a_own[3, xo, ROWS_A:512].astype(F32) + yb_full[0, xo].astype(F32) + yb_full[1, xo].astype(F32)
        ).astype(BF16)

    add_a(0)
    for dr in range(2):
        a_half(dr).start()
    for dr in range(2):
        send_b(dr, x)
    forward(0, 2, 0)
    forward(0, 2, 1)
    sum_b(1 - x)
    bx().start()
    forward(0, 3, 0)
    send_a(0)
    send_a(1)
    forward(0, 3, 1)
    add_a(3)
    forward(0, 4, 0)
    forward(0, 4, 1)
    forward(1, 2, 1)
    forward(1, 3, 0)
    sum_b(x)
    a_full(0).wait_recv()
    a_full(1).wait_recv()
    pltpu.make_async_copy(resid, resid, sem_res).wait()

    def finish(lo, hi, total):
        hidden = total + res_v[lo // 32 : hi // 32].astype(F32).reshape(hi - lo, 512)
        hg[lo:hi] = (hidden * gain[...].astype(F32).reshape(1, 512)).astype(BF16)
        sq = hidden * hidden
        sq = sq[:, 0:128] + sq[:, 128:256] + sq[:, 256:384] + sq[:, 384:512]
        pw[lo // 32 : hi // 32] = sq.reshape((hi - lo) // 32, 32, 128)

    finish(0, ROWS_A, a_own[3, x, 0:ROWS_A].astype(F32) + ya_full[0].astype(F32) + ya_full[1].astype(F32))
    bx().wait_recv()
    finish(ROWS_A, 512, a_own[3, x, ROWS_A:512].astype(F32) + xb_recv[...].astype(F32))

    def power(i):
        to = (t + i) % 16
        return remote(
            pw.at[to % 2 * 8 + to // 8 * 4 + to // 2 % 4], pw_recv.at[i], pw_s, pw_r, (s, to)
        )

    def send_power(i, carry):
        power(i).start()
        return carry

    lax.fori_loop(1, 16, send_power, 0)

    def root():
        whole(pw_recv.at[pl.ds(1, 15)], pw_s, pw_r).wait_recv()

        def one(i, total):
            return total + pw_recv[i]

        total = lax.fori_loop(1, 16, one, pw[c * 8 + x * 4 + y])
        mean = jnp.sum(total, axis=1, keepdims=True) * (1.0 / 8192)
        r_v[...] = jnp.broadcast_to(lax.rsqrt(mean + 1e-05), (32, 256))

    pltpu.make_async_copy(student, stu_v, sem_stu).wait()
    arrived(0, 4, 0)
    arrived(0, 4, 1)

    def block(q, m):
        line = (q + 3 + 2 * m) // 8
        off = (1 - 2 * m) * (4 - q - m + 4 * line)
        return (xh + 1 + line) % 2 * 8 + (z + off + 8) % 8

    def ds_(k, i):
        return d_s.at[k % 2, i], d_r.at[k % 8, i]

    def dc(k):
        return remote(t_send.at[k], t_crecv.at[k], *ds_(k, 0), sib)

    def dx(g, m):
        k = 2 * g + m
        if m == 0:
            return remote(t_own.at[k, 1 - x], xr0.at[g], *ds_(k, 1), xdev)
        return remote(t_own.at[k, 1 - x, y], xr1.at[g], *ds_(k, 1), xdev)

    def dy(g, m, o):
        k = 2 * g + m
        if m == 0:
            return remote(t_own.at[k, x, (y + o) % 4], yr0.at[g, o - 1], *ds_(k, 2), ydev(o))
        return remote(t_own.at[k, :, (y + o) % 4], yr1.at[g, o - 1], *ds_(k, 2), ydev(o))

    def ex(g, m):
        k = 2 * g + m
        ref = m_all.at[k, c, x] if m == 0 else m_all.at[k, c, x, y]
        return remote(ref, ref, *ds_(k, 3), xdev)

    def ey(g, m, o):
        k = 2 * g + m
        ref = m_all.at[k, c, x, y] if m == 0 else m_all.at[k, c, :, y]
        return remote(ref, ref, *ds_(k, 4), ydev(o))

    def y_arrived(g, m, i):
        whole(yr0.at[g] if m == 0 else yr1.at[g], *ds_(2 * g + m, i)).wait_recv()

    def ec(k):
        return remote(m_all.at[k, c], m_all.at[k, c], *ds_(k, 5), sib)

    def fz(line, dr, j, p, k):
        cols = pl.ds(256 * p, 256)
        return remote(
            g_send.at[k, :, cols], ring.at[line, dr, j, :, cols], f_s, f_r.at[line, dr, j, p],
            zdev[dr],
        )

    def fz_half(line, dr, p, k):
        rows, cols = pl.ds(128 * dr, 128), pl.ds(256 * p, 256)
        return remote(
            g_send.at[k, rows, cols], ring.at[line, dr, 0, rows, cols], f_s,
            f_r.at[line, dr, 0, p], zdev[dr],
        )

    def fx(p):
        cols = pl.ds(256 * p, 256)
        return remote(g_send.at[8, :, cols], rx.at[:, cols], fx_s, fx_r.at[p], xhdev)

    def core_rows(co):
        return pl.ds(pl.multiple_of(co * 256, 256), 256)

    def stage0(g, m):
        k = 2 * g + m
        b = block(g, m)
        t_send[k] = dot(hg[core_rows(1 - c)], pj[b]).astype(BF16).reshape(2, 4, 32, 256)
        dc(k).start()
        t_own[k] = dot(hg[core_rows(c)], pj[b]).astype(BF16).reshape(2, 4, 32, 256)

    def stage1(g, m):
        k = 2 * g + m
        dc(k).wait_recv()
        t_own[k] = (t_own[k].astype(F32) + t_crecv[k].astype(F32)).astype(BF16)
        if m == 0:
            dx(g, m).start()
        else:
            for o in (2, 1, 3):
                dy(g, m, o).start()

    def stage2(g, m):
        k = 2 * g + m
        if m == 0:
            dx(g, m).wait_recv()
            t_own[k, x] = (t_own[k, x].astype(F32) + xr0[g].astype(F32)).astype(BF16)
            for o in (2, 1, 3):
                dy(g, m, o).start()
        else:
            total = t_own[k, :, y].astype(F32)
            y_arrived(g, m, 2)
            for o in range(3):
                total = total + yr1[g, o].astype(F32)
            t_own[k, :, y] = total.astype(BF16)
            dx(g, m).start()

    def stage3(g, m):
        k = 2 * g + m
        if m == 0:
            total = t_own[k, x, y].astype(F32)
            y_arrived(g, m, 2)
            for o in range(3):
                total = total + yr0[g, o].astype(F32)
        else:
            dx(g, m).wait_recv()
            total = t_own[k, x, y].astype(F32) + xr1[g].astype(F32)
        cols = pl.ds(pl.multiple_of(block(g, m) * 256, 256), 256)
        mismatch = total * r_v[...] - stu_v[:, cols].astype(F32)
        mis_v[:, cols] = mismatch
        m_all[k, c, x, y] = (mismatch * r_v[...]).astype(BF16)
        if m == 0:
            for o in (2, 1, 3):
                ey(g, m, o).start()
        else:
            ex(g, m).start()

    def stage4(g, m):
        if m == 0:
            y_arrived(g, m, 4)
            ex(g, m).start()
        else:
            ex(g, m).wait_recv()
            for o in (2, 1, 3):
                ey(g, m, o).start()

    def stage5(g, m):
        if m == 0:
            ex(g, m).wait_recv()
        else:
            y_arrived(g, m, 4)
        ec(2 * g + m).start()

    def put_grad(p):
        cols = pl.ds(256 * p, 256)
        return pltpu.make_async_copy(grad_v.at[:, cols], grad_out.at[:, cols], sem_grad.at[p])

    def put_mis():
        return pltpu.make_async_copy(mis_v, mis_out, sem_mis)

    def stage6(q, m):
        k = 2 * q + m
        ec(k).wait_recv()
        g_acc[m] = dot(m_all[k].reshape(512, 256), hg[...], ((0,), (0,)))
        reduce(q, m, 0)

    def stage7(q, m):
        reduce(q, m, 1)

    def reduce(q, m, p):
        k = 2 * q + m
        cols = slice(256 * p, 256 * p + 256)
        part = g_acc[m, :, cols]

        @pl.when(q == 3 * m)
        def _():
            g_send[k, :, cols] = part.astype(BF16)
            fz_half(m, 0, p, k).start()
            fz_half(m, 1, p, k).start()

        @pl.when(q == 4 + 3 * m)
        def _():
            for dr in range(2):
                fz(m, dr, 3, p, k).wait_recv()
            total = part + ring[m, 0, 3, :, cols].astype(F32) + ring[m, 1, 3, :, cols].astype(F32)
            if m == 0:
                g_send[k, :, cols] = total.astype(BF16)
                fx(p).start()
            else:
                fx(p).wait_recv()
                grad_v[:, cols] = (total + rx[:, cols].astype(F32)) * (1.0 / math.sqrt(8192))
                put_grad(p).start()

        @pl.when((q != 3 * m) & (q != 4 + 3 * m))
        def _():
            line = (q + 3 + 2 * m) // 8
            j = q + m - 1 - 4 * line

            @pl.when(j == 0)
            def _():
                fz_half(line, m, p, k).wait_recv()

            @pl.when(j > 0)
            def _():
                fz(line, m, j, p, k).wait_recv()

            g_send[k, :, cols] = (part + ring[line, m, j, :, cols].astype(F32)).astype(BF16)
            fz(line, m, j + 1, p, k).start()

    stages = (stage0, stage1, stage2, stage3, stage4, stage5, stage6, stage7)

    def student_steps(h, carry):
        for par in range(2):
            for n in reversed(range(len(stages))):
                m = (par - STEPS[n]) % 2
                q = h + (par - STEPS[n] - m) // 2
                pl.when((q >= 0) & (q < BLOCKS))(lambda: stages[n](q, m))

            if par == 0:

                @pl.when(h == 0)
                def _():
                    forward(1, 3, 1)

                @pl.when(h == 2)
                def _():
                    root()
                    forward(1, 4, 0)
                    forward(1, 4, 1)

                @pl.when(h == 3)
                def _():
                    arrived(1, 4, 0)
                    arrived(1, 4, 1)

                @pl.when(h == 11)
                def _():
                    put_mis().start()

        return carry

    lax.fori_loop(0, BLOCKS + (STEPS[-1] + 1) // 2, student_steps, 0)

    for ref, sem in (
        (pj.at[s], cx_s), (pj.at[pl.ds(0, 14)], cz_s), (a_send, ac_s), (a_xrecv, ax_s), (ya_half, ay_s.at[0]),
        (ya_full, ay_s.at[1]), (yb_half, by_s.at[0]), (yb_full, by_s.at[1]), (xb_recv, bx_s),
        (pw_recv.at[pl.ds(1, 15)], pw_s), (g_send.at[pl.ds(0, 14)], f_s), (rx, fx_s),
        (t_send.at[pl.ds(0, 8)], d_s.at[0, 0]), (t_send.at[pl.ds(0, 8)], d_s.at[1, 0]),
        (xr0, d_s.at[0, 1]), (xr1, d_s.at[1, 1]), (yr0, d_s.at[0, 2]), (yr1, d_s.at[1, 2]),
        (xr0, d_s.at[0, 3]), (xr1, d_s.at[1, 3]), (yr0, d_s.at[0, 4]), (yr1, d_s.at[1, 4]),
        (t_send.at[pl.ds(0, 8)], d_s.at[0, 5]), (t_send.at[pl.ds(0, 8)], d_s.at[1, 5]),
    ):
        whole(ref, sem, pw_r).wait_send()
    put_mis().wait()
    put_grad(0).wait()
    put_grad(1).wait()


def shards(attn_heads, out_weight, residual, norm_gain, proj, student_hidden):
    hbm = pl.BlockSpec(memory_space=pl.ANY)
    vmem = pl.BlockSpec(memory_space=pltpu.VMEM)
    buf = lambda *shape: pltpu.VMEM(shape, BF16)
    dma = lambda *shape: pltpu.SemaphoreType.DMA(shape)
    return pl.pallas_call(
        kernel,
        name="distill",
        out_shape=(
            jax.ShapeDtypeStruct((32, 4096), F32),
            jax.ShapeDtypeStruct((256, 512), F32),
        ),
        in_specs=[hbm, hbm, hbm, vmem, hbm, hbm],
        out_specs=(hbm, hbm),
        scratch_shapes=[
            buf(16, 32, 512), buf(16, 32, 512), buf(8, 512, 1024), buf(32, 4096),
            buf(4, 2, 512, 512), buf(4, 2, 512, 512), buf(4, 2, 512, 512), buf(4, ROWS_A, 512),
            buf(2, HALF_A, 512), buf(2, ROWS_A, 512), buf(2, 2, HALF_B, 512), buf(2, 2, 2 * HALF_B, 512),
            buf(2 * HALF_B, 512),
            buf(512, 512), pltpu.VMEM((16, 32, 128), F32), pltpu.VMEM((16, 32, 128), F32),
            pltpu.VMEM((32, 256), F32),
            buf(16, 512, 256),
            buf(16, 2, 4, 32, 256), buf(16, 2, 4, 32, 256), buf(16, 2, 4, 32, 256),
            buf(8, 4, 32, 256), buf(8, 3, 32, 256), buf(8, 3, 2, 32, 256), buf(8, 32, 256),
            buf(16, 2, 2, 4, 32, 256),
            pltpu.VMEM((2, 256, 512), F32), buf(16, 256, 512), buf(2, 2, 4, 256, 512), buf(256, 512),
            pltpu.VMEM((32, 4096), F32), pltpu.VMEM((256, 512), F32),
            dma(), dma(), dma(), dma(8), dma(), dma(), dma(2),
            dma(), dma(4, 2), dma(), dma(4), dma(2), dma(2, 2), dma(2), dma(2, 2, 2), dma(), dma(),
            dma(), dma(), dma(), dma(), dma(), dma(2, 2, 4, 2),
            dma(2, 6), dma(8, 6), dma(), dma(2, 2, 4, 2), dma(), dma(2),
        ],
        compiler_params=pltpu.CompilerParams(
            collective_id=0, has_side_effects=True, vmem_limit_bytes=62 * 2**20
        ),
    )(attn_heads, out_weight, residual, norm_gain, proj, student_hidden)


def solution(mesh):
    return jax.shard_map(
        shards,
        mesh=mesh,
        in_specs=(
            P("seq", "tensor"),
            P("tensor", None),
            P("seq", "tensor"),
            P("tensor"),
            P("tensor", "seq"),
            P(("seq", "tensor"), None),
        ),
        out_specs=(P(("seq", "tensor"), None), P("seq", "tensor")),
        check_vma=False,
    )
```

```python
import math

import jax
import jax.numpy as jnp
from jax import lax
from jax.experimental import pallas as pl
from jax.experimental.pallas import tpu as pltpu
from jax.sharding import PartitionSpec as P

MESH = pl.DeviceIdType.MESH
F32 = jnp.float32
BF16 = jnp.bfloat16
BLOCKS = 8
STEPS = (0, 1, 3, 5, 7, 9, 10, 11)
ROWS_A = 160
HALF_A, HALF_B = ROWS_A // 2, (512 - ROWS_A) // 2


def dot(a, b, dims=((1,), (0,))):
    return lax.dot_general(a, b, (dims, ((), ())), preferred_element_type=F32)


def kernel(
    attn, weight, resid, gain, proj, student,
    mis_out, grad_out,
    attn_v, res_v, w_v, stu_v,
    a_send, a_own, a_crecv, a_xrecv, ya_half, ya_full, yb_half, yb_full, xb_recv,
    hg, pw, pw_recv, r_v,
    pj,
    t_send, t_own, t_crecv, xr0, yr0, yr1, xr1, m_all,
    g_acc, g_send, ring, rx,
    sem_attn, sem_res, sem_stu, sem_w, sem_proj,
    ac_s, ac_r, ax_s, ax_r, ay_s, ay_r, by_s, by_r, bx_s, bx_r,
    pw_s, pw_r, cx_s, cx_r, cz_s, cz_r,
    d_s, d_r, f_s, f_r, fx_s, fx_r,
):
    s = lax.axis_index("seq")
    t = lax.axis_index("tensor")
    xh, z = s // 8, s % 8
    x, y, c = t // 8, (t // 2) % 4, t % 2

    def at(xh_, z_, x_, y_, c_):
        return (xh_ * 8 + z_, x_ * 8 + y_ * 2 + c_)

    sib = at(xh, z, x, y, 1 - c)
    xdev = at(xh, z, 1 - x, y, c)
    xhdev = at(1 - xh, z, x, y, c)
    zdev = (at(xh, (z + 1) % 8, x, y, c), at(xh, (z + 7) % 8, x, y, c))

    def ydev(o):
        return at(xh, z, x, (y + o) % 4, c)

    def remote(src, dst, ss, rs, dev):
        return pltpu.make_async_remote_copy(
            src_ref=src, dst_ref=dst, send_sem=ss, recv_sem=rs, device_id=dev, device_id_type=MESH
        )

    barrier = pltpu.get_barrier_semaphore()

    def greet(i, carry):
        pl.semaphore_signal(barrier, inc=1, device_id=(s, (t + i) % 16), device_id_type=MESH)
        return carry

    lax.fori_loop(1, 16, greet, 0)
    for dev in (xhdev,) + zdev:
        pl.semaphore_signal(barrier, inc=1, device_id=dev, device_id_type=MESH)

    def whole(ref, ss, rs):
        return remote(ref, ref, ss, rs, sib)

    def tokens(i):
        return (i % 8) // 4 * 8 + (i % 4) * 2 + i // 8

    def load_rows(src, dst, sem):
        def one(i, carry):
            row = pl.multiple_of(tokens(i) * 32, 32)
            pltpu.make_async_copy(src.at[pl.ds(row, 32)], dst.at[i], sem).start()
            return carry

        lax.fori_loop(0, 16, one, 0)

    def block_of(j, xo, co):
        dy = 2 - j + (j // 2) * (3 - 2 * (j % 2))
        return xo * 8 + (y + dy) % 4 * 2 + co

    def load_w(u):
        b = block_of(u // 2, (x + 1 + u % 2) % 2, 0) // 2
        col = pl.multiple_of(b * 1024, 1024)
        return pltpu.make_async_copy(weight.at[:, pl.ds(col, 1024)], w_v.at[u], sem_w.at[u])

    pltpu.make_async_copy(proj, pj.at[s], sem_proj).start()
    load_rows(attn, attn_v, sem_attn)
    for u in range(8):
        load_w(u).start()
    load_rows(resid, res_v, sem_res)
    pltpu.make_async_copy(student, stu_v, sem_stu).start()

    ring[:, 0, 0, 128:256] = jnp.zeros((2, 128, 512), BF16)
    ring[:, 1, 0, 0:128] = jnp.zeros((2, 128, 512), BF16)

    pl.semaphore_wait(barrier, 18)

    def cz(line, dr, j, p):
        sign = 1 - 2 * dr
        xx = xh if line == 1 else 1 - xh
        b = xx * 8 + (z - sign * (j - 1) + 8) % 8
        if j == 4:
            ref = pj.at[b, pl.ds(256 * dr + 128 * p, 128)]
        else:
            ref = pj.at[b, pl.ds(256 * p, 256)]
        return remote(ref, ref, cz_s, cz_r.at[line, dr, j - 1, p], zdev[dr])

    def cx():
        return remote(pj.at[s], pj.at[s], cx_s, cx_r, xhdev)

    def arrived(line, j, p):
        for dr in range(2):
            if j == 3:
                if p == 0:
                    cz(line, dr, j, 0).wait_recv()
                    cz(line, dr, j, 1).wait_recv()
            else:
                cz(line, dr, j, p).wait_recv()

    def forward(line, j, p):
        if j > 1:
            arrived(line, j - 1, p)
        for dr in range(2):
            cz(line, dr, j, p).start()

    pltpu.make_async_copy(proj, pj.at[s], sem_proj).wait()
    cx().start()
    forward(1, 1, 0)
    forward(1, 1, 1)

    def ac(j, xo):
        return remote(a_send.at[j, xo], a_crecv.at[j, xo], ac_s, ac_r.at[j, xo], sib)

    def ax(j):
        return remote(a_own.at[j, 1 - x, pl.ds(0, ROWS_A)], a_xrecv.at[j], ax_s, ax_r.at[j], xdev)

    def a_half(dr):
        return remote(
            a_own.at[0, x, pl.ds(HALF_A * dr, HALF_A)], ya_half.at[dr], ay_s.at[0], ay_r.at[0, dr], ydev(1 + 2 * dr)
        )

    def a_full(dr):
        return remote(
            a_own.at[1 + dr, x, pl.ds(0, ROWS_A)], ya_full.at[dr], ay_s.at[1], ay_r.at[1, dr], ydev(1 + 2 * dr)
        )

    def b_half(dr, xo):
        return remote(
            a_own.at[0, xo, pl.ds(ROWS_A + HALF_B * dr, HALF_B)], yb_half.at[dr, xo], by_s.at[0], by_r.at[0, dr, xo],
            ydev(1 + 2 * dr),
        )

    def b_full(dr, xo):
        return remote(
            a_own.at[1 + dr, xo, pl.ds(ROWS_A, 2 * HALF_B)], yb_full.at[dr, xo], by_s.at[1], by_r.at[1, dr, xo],
            ydev(1 + 2 * dr),
        )

    def bx():
        return remote(a_own.at[3, 1 - x, pl.ds(ROWS_A, 2 * HALF_B)], xb_recv, bx_s, bx_r, xdev)

    def product(u, co, out):
        j, xo = unit(u)
        cols = pl.ds(pl.multiple_of(co * 512, 512), 512)
        out[j, xo] = dot(attn_v[...].reshape(512, 512), w_v[u, :, cols]).astype(BF16)

    def unit(u):
        return u // 2, (x + 1 + u % 2) % 2

    def multiply(u):
        j, xo = unit(u)
        load_w(u).wait()
        product(u, 1 - c, a_send)
        ac(j, xo).start()
        product(u, c, a_own)

    def combine(u):
        j, xo = unit(u)
        ac(j, xo).wait_recv()
        a_own[j, xo] = (a_own[j, xo].astype(F32) + a_crecv[j, xo].astype(F32)).astype(BF16)

        @pl.when(u % 2 == 0)
        def _():
            ax(j).start()

        @pl.when(u < 2)
        def _():
            b_half(0, xo).start()
            b_half(1, xo).start()

    def send_b(dr, xo):
        rows = slice(ROWS_A + HALF_B * dr, ROWS_A + HALF_B * dr + HALF_B)
        b_half(dr, xo).wait_recv()
        a_own[1 + dr, xo, rows] = (a_own[1 + dr, xo, rows].astype(F32) + yb_half[dr, xo].astype(F32)).astype(BF16)
        b_full(dr, xo).start()

    def add_a(j):
        ax(j).wait_recv()
        a_own[j, x, 0:ROWS_A] = (a_own[j, x, 0:ROWS_A].astype(F32) + a_xrecv[j].astype(F32)).astype(BF16)

    pltpu.make_async_copy(attn, attn, sem_attn).wait()

    def teacher(u, carry):
        @pl.when(u < 8)
        def _():
            multiply(u)

        @pl.when(u >= 1)
        def _():
            combine(u - 1)

        @pl.when(u == 6)
        def _():
            forward(1, 2, 0)

        @pl.when(u == 7)
        def _():
            send_b(0, 1 - x)
            send_b(1, 1 - x)
            cx().wait_recv()
            forward(0, 1, 0)
            forward(0, 1, 1)

        return carry

    lax.fori_loop(0, 9, teacher, 0)

    def send_a(dr):
        rows = slice(HALF_A * dr, HALF_A * dr + HALF_A)
        add_a(1 + dr)
        a_half(dr).wait_recv()
        a_own[1 + dr, x, rows] = (a_own[1 + dr, x, rows].astype(F32) + ya_half[dr].astype(F32)).astype(BF16)
        a_full(dr).start()

    def sum_b(xo):
        b_full(0, xo).wait_recv()
        b_full(1, xo).wait_recv()
        a_own[3, xo, ROWS_A:512] = (
            a_own[3, xo, ROWS_A:512].astype(F32) + yb_full[0, xo].astype(F32) + yb_full[1, xo].astype(F32)
        ).astype(BF16)

    add_a(0)
    for dr in range(2):
        a_half(dr).start()
    for dr in range(2):
        send_b(dr, x)
    forward(0, 2, 0)
    forward(0, 2, 1)
    sum_b(1 - x)
    bx().start()
    forward(0, 3, 0)
    send_a(0)
    send_a(1)
    forward(0, 3, 1)
    add_a(3)
    forward(0, 4, 0)
    forward(0, 4, 1)
    forward(1, 2, 1)
    forward(1, 3, 0)
    sum_b(x)
    a_full(0).wait_recv()
    a_full(1).wait_recv()
    pltpu.make_async_copy(resid, resid, sem_res).wait()

    def finish(lo, hi, total):
        hidden = total + res_v[lo // 32 : hi // 32].astype(F32).reshape(hi - lo, 512)
        hg[lo:hi] = (hidden * gain[...].astype(F32).reshape(1, 512)).astype(BF16)
        sq = hidden * hidden
        sq = sq[:, 0:128] + sq[:, 128:256] + sq[:, 256:384] + sq[:, 384:512]
        pw[lo // 32 : hi // 32] = sq.reshape((hi - lo) // 32, 32, 128)

    finish(0, ROWS_A, a_own[3, x, 0:ROWS_A].astype(F32) + ya_full[0].astype(F32) + ya_full[1].astype(F32))
    bx().wait_recv()
    finish(ROWS_A, 512, a_own[3, x, ROWS_A:512].astype(F32) + xb_recv[...].astype(F32))

    def power(i):
        to = (t + i) % 16
        return remote(
            pw.at[to % 2 * 8 + to // 8 * 4 + to // 2 % 4], pw_recv.at[i], pw_s, pw_r, (s, to)
        )

    def send_power(i, carry):
        power(i).start()
        return carry

    lax.fori_loop(1, 16, send_power, 0)

    def root():
        whole(pw_recv.at[pl.ds(1, 15)], pw_s, pw_r).wait_recv()

        def one(i, total):
            return total + pw_recv[i]

        total = lax.fori_loop(1, 16, one, pw[c * 8 + x * 4 + y])
        mean = jnp.sum(total, axis=1, keepdims=True) * (1.0 / 8192)
        r_v[...] = jnp.broadcast_to(lax.rsqrt(mean + 1e-05), (32, 256))

    pltpu.make_async_copy(student, stu_v, sem_stu).wait()
    arrived(0, 4, 0)
    arrived(0, 4, 1)

    def block(q, m):
        line = (q + 3 + 2 * m) // 8
        off = (1 - 2 * m) * (4 - q - m + 4 * line)
        return (xh + 1 + line) % 2 * 8 + (z + off + 8) % 8

    def ds_(k, i):
        return d_s.at[k % 2, i], d_r.at[k % 8, i]

    def dc(k):
        return remote(t_send.at[k], t_crecv.at[k], *ds_(k, 0), sib)

    def dx(g, m):
        k = 2 * g + m
        if m == 0:
            return remote(t_own.at[k, 1 - x], xr0.at[g], *ds_(k, 1), xdev)
        return remote(t_own.at[k, 1 - x, y], xr1.at[g], *ds_(k, 1), xdev)

    def dy(g, m, o):
        k = 2 * g + m
        if m == 0:
            return remote(t_own.at[k, x, (y + o) % 4], yr0.at[g, o - 1], *ds_(k, 2), ydev(o))
        return remote(t_own.at[k, :, (y + o) % 4], yr1.at[g, o - 1], *ds_(k, 2), ydev(o))

    def ex(g, m):
        k = 2 * g + m
        ref = m_all.at[k, c, x] if m == 0 else m_all.at[k, c, x, y]
        return remote(ref, ref, *ds_(k, 3), xdev)

    def ey(g, m, o):
        k = 2 * g + m
        ref = m_all.at[k, c, x, y] if m == 0 else m_all.at[k, c, :, y]
        return remote(ref, ref, *ds_(k, 4), ydev(o))

    def y_arrived(g, m, i):
        whole(yr0.at[g] if m == 0 else yr1.at[g], *ds_(2 * g + m, i)).wait_recv()

    def ec(k):
        return remote(m_all.at[k, c], m_all.at[k, c], *ds_(k, 5), sib)

    def fz(line, dr, j, p, k):
        cols = pl.ds(256 * p, 256)
        return remote(
            g_send.at[k, :, cols], ring.at[line, dr, j, :, cols], f_s, f_r.at[line, dr, j, p],
            zdev[dr],
        )

    def fz_half(line, dr, p, k):
        rows, cols = pl.ds(128 * dr, 128), pl.ds(256 * p, 256)
        return remote(
            g_send.at[k, rows, cols], ring.at[line, dr, 0, rows, cols], f_s,
            f_r.at[line, dr, 0, p], zdev[dr],
        )

    def fx(p):
        cols = pl.ds(256 * p, 256)
        return remote(g_send.at[8, :, cols], rx.at[:, cols], fx_s, fx_r.at[p], xhdev)

    def core_rows(co):
        return pl.ds(pl.multiple_of(co * 256, 256), 256)

    def stage0(g, m):
        k = 2 * g + m
        b = block(g, m)
        t_send[k] = dot(hg[core_rows(1 - c)], pj[b]).astype(BF16).reshape(2, 4, 32, 256)
        dc(k).start()
        t_own[k] = dot(hg[core_rows(c)], pj[b]).astype(BF16).reshape(2, 4, 32, 256)

    def stage1(g, m):
        k = 2 * g + m
        dc(k).wait_recv()
        t_own[k] = (t_own[k].astype(F32) + t_crecv[k].astype(F32)).astype(BF16)
        if m == 0:
            dx(g, m).start()
        else:
            for o in (2, 1, 3):
                dy(g, m, o).start()

    def stage2(g, m):
        k = 2 * g + m
        if m == 0:
            dx(g, m).wait_recv()
            t_own[k, x] = (t_own[k, x].astype(F32) + xr0[g].astype(F32)).astype(BF16)
            for o in (2, 1, 3):
                dy(g, m, o).start()
        else:
            total = t_own[k, :, y].astype(F32)
            y_arrived(g, m, 2)
            for o in range(3):
                total = total + yr1[g, o].astype(F32)
            t_own[k, :, y] = total.astype(BF16)
            dx(g, m).start()

    def stage3(g, m):
        k = 2 * g + m
        if m == 0:
            total = t_own[k, x, y].astype(F32)
            y_arrived(g, m, 2)
            for o in range(3):
                total = total + yr0[g, o].astype(F32)
        else:
            dx(g, m).wait_recv()
            total = t_own[k, x, y].astype(F32) + xr1[g].astype(F32)
        cols = pl.ds(pl.multiple_of(block(g, m) * 256, 256), 256)
        mismatch = total * r_v[...] - stu_v[:, cols].astype(F32)
        mis_out[:, cols] = mismatch
        m_all[k, c, x, y] = (mismatch * r_v[...]).astype(BF16)
        if m == 0:
            for o in (2, 1, 3):
                ey(g, m, o).start()
        else:
            ex(g, m).start()

    def stage4(g, m):
        if m == 0:
            y_arrived(g, m, 4)
            ex(g, m).start()
        else:
            ex(g, m).wait_recv()
            for o in (2, 1, 3):
                ey(g, m, o).start()

    def stage5(g, m):
        if m == 0:
            ex(g, m).wait_recv()
        else:
            y_arrived(g, m, 4)
        ec(2 * g + m).start()

    def stage6(q, m):
        k = 2 * q + m
        ec(k).wait_recv()
        g_acc[m] = dot(m_all[k].reshape(512, 256), hg[...], ((0,), (0,)))
        reduce(q, m, 0)

    def stage7(q, m):
        reduce(q, m, 1)

    def reduce(q, m, p):
        k = 2 * q + m
        cols = slice(256 * p, 256 * p + 256)
        part = g_acc[m, :, cols]

        @pl.when(q == 3 * m)
        def _():
            g_send[k, :, cols] = part.astype(BF16)
            fz_half(m, 0, p, k).start()
            fz_half(m, 1, p, k).start()

        @pl.when(q == 4 + 3 * m)
        def _():
            for dr in range(2):
                fz(m, dr, 3, p, k).wait_recv()
            total = part + ring[m, 0, 3, :, cols].astype(F32) + ring[m, 1, 3, :, cols].astype(F32)
            if m == 0:
                g_send[k, :, cols] = total.astype(BF16)
                fx(p).start()
            else:
                fx(p).wait_recv()
                grad_out[:, cols] = (total + rx[:, cols].astype(F32)) * (1.0 / math.sqrt(8192))

        @pl.when((q != 3 * m) & (q != 4 + 3 * m))
        def _():
            line = (q + 3 + 2 * m) // 8
            j = q + m - 1 - 4 * line

            @pl.when(j == 0)
            def _():
                fz_half(line, m, p, k).wait_recv()

            @pl.when(j > 0)
            def _():
                fz(line, m, j, p, k).wait_recv()

            g_send[k, :, cols] = (part + ring[line, m, j, :, cols].astype(F32)).astype(BF16)
            fz(line, m, j + 1, p, k).start()

    stages = (stage0, stage1, stage2, stage3, stage4, stage5, stage6, stage7)

    def student_steps(h, carry):
        for par in range(2):
            for n in reversed(range(len(stages))):
                m = (par - STEPS[n]) % 2
                q = h + (par - STEPS[n] - m) // 2
                pl.when((q >= 0) & (q < BLOCKS))(lambda: stages[n](q, m))

            if par == 0:

                @pl.when(h == 0)
                def _():
                    forward(1, 3, 1)

                @pl.when(h == 2)
                def _():
                    root()
                    forward(1, 4, 0)
                    forward(1, 4, 1)

                @pl.when(h == 3)
                def _():
                    arrived(1, 4, 0)
                    arrived(1, 4, 1)

        return carry

    lax.fori_loop(0, BLOCKS + (STEPS[-1] + 1) // 2, student_steps, 0)

    for ref, sem in (
        (pj.at[s], cx_s), (pj.at[pl.ds(0, 14)], cz_s), (a_send, ac_s), (a_xrecv, ax_s), (ya_half, ay_s.at[0]),
        (ya_full, ay_s.at[1]), (yb_half, by_s.at[0]), (yb_full, by_s.at[1]), (xb_recv, bx_s),
        (pw_recv.at[pl.ds(1, 15)], pw_s), (g_send.at[pl.ds(0, 14)], f_s), (rx, fx_s),
        (t_send.at[pl.ds(0, 8)], d_s.at[0, 0]), (t_send.at[pl.ds(0, 8)], d_s.at[1, 0]),
        (xr0, d_s.at[0, 1]), (xr1, d_s.at[1, 1]), (yr0, d_s.at[0, 2]), (yr1, d_s.at[1, 2]),
        (xr0, d_s.at[0, 3]), (xr1, d_s.at[1, 3]), (yr0, d_s.at[0, 4]), (yr1, d_s.at[1, 4]),
        (t_send.at[pl.ds(0, 8)], d_s.at[0, 5]), (t_send.at[pl.ds(0, 8)], d_s.at[1, 5]),
    ):
        whole(ref, sem, pw_r).wait_send()


def shards(attn_heads, out_weight, residual, norm_gain, proj, student_hidden):
    hbm = pl.BlockSpec(memory_space=pl.ANY)
    vmem = pl.BlockSpec(memory_space=pltpu.VMEM)
    buf = lambda *shape: pltpu.VMEM(shape, BF16)
    dma = lambda *shape: pltpu.SemaphoreType.DMA(shape)
    return pl.pallas_call(
        kernel,
        name="distill",
        out_shape=(
            pltpu.VMEM((32, 4096), F32),
            pltpu.VMEM((256, 512), F32),
        ),
        in_specs=[hbm, hbm, hbm, vmem, hbm, hbm],
        out_specs=(vmem, vmem),
        scratch_shapes=[
            buf(16, 32, 512), buf(16, 32, 512), buf(8, 512, 1024), buf(32, 4096),
            buf(4, 2, 512, 512), buf(4, 2, 512, 512), buf(4, 2, 512, 512), buf(4, ROWS_A, 512),
            buf(2, HALF_A, 512), buf(2, ROWS_A, 512), buf(2, 2, HALF_B, 512), buf(2, 2, 2 * HALF_B, 512),
            buf(2 * HALF_B, 512),
            buf(512, 512), pltpu.VMEM((16, 32, 128), F32), pltpu.VMEM((16, 32, 128), F32),
            pltpu.VMEM((32, 256), F32),
            buf(16, 512, 256),
            buf(16, 2, 4, 32, 256), buf(16, 2, 4, 32, 256), buf(16, 2, 4, 32, 256),
            buf(8, 4, 32, 256), buf(8, 3, 32, 256), buf(8, 3, 2, 32, 256), buf(8, 32, 256),
            buf(16, 2, 2, 4, 32, 256),
            pltpu.VMEM((2, 256, 512), F32), buf(16, 256, 512), buf(2, 2, 4, 256, 512), buf(256, 512),
            dma(), dma(), dma(), dma(8), dma(),
            dma(), dma(4, 2), dma(), dma(4), dma(2), dma(2, 2), dma(2), dma(2, 2, 2), dma(), dma(),
            dma(), dma(), dma(), dma(), dma(), dma(2, 2, 4, 2),
            dma(2, 6), dma(8, 6), dma(), dma(2, 2, 4, 2), dma(), dma(2),
        ],
        compiler_params=pltpu.CompilerParams(
            collective_id=0, has_side_effects=True, vmem_limit_bytes=62 * 2**20
        ),
    )(attn_heads, out_weight, residual, norm_gain, proj, student_hidden)


def solution(mesh):
    return jax.shard_map(
        shards,
        mesh=mesh,
        in_specs=(
            P("seq", "tensor"),
            P("tensor", None),
            P("seq", "tensor"),
            P("tensor"),
            P("tensor", "seq"),
            P(("seq", "tensor"), None),
        ),
        out_specs=(P(("seq", "tensor"), None), P("seq", "tensor")),
        check_vma=False,
    )
```

```python
import math

import jax
import jax.numpy as jnp
from jax import lax
from jax.experimental import pallas as pl
from jax.experimental.pallas import tpu as pltpu
from jax.sharding import PartitionSpec as P

MESH = pl.DeviceIdType.MESH
F32 = jnp.float32
BF16 = jnp.bfloat16
BLOCKS = 8
STEPS = (0, 0, 2, 4, 6, 8, 8, 9)
ROWS_A = 160
HALF_A, HALF_B = ROWS_A // 2, (512 - ROWS_A) // 2


def dot(a, b, dims=((1,), (0,))):
    return lax.dot_general(a, b, (dims, ((), ())), preferred_element_type=F32)


def kernel(
    attn, weight, resid, gain, proj, student,
    mis_out, grad_out,
    attn_v, res_v, w_v, stu_v,
    a_send, a_own, a_crecv, a_xrecv, ya_half, ya_full, yb_half, yb_full, xb_recv,
    hg, pw, pw_recv, r_v,
    pj,
    t_send, t_own, t_crecv, xr0, yr0, yr1, xr1, m_all,
    g_acc, g_send, ring, rx,
    sem_attn, sem_res, sem_stu, sem_w, sem_proj,
    ac_s, ac_r, ax_s, ax_r, ay_s, ay_r, by_s, by_r, bx_s, bx_r,
    pw_s, pw_r, cx_s, cx_r, cz_s, cz_r,
    d_s, d_r, f_s, f_r, fx_s, fx_r,
):
    s = lax.axis_index("seq")
    t = lax.axis_index("tensor")
    xh, z = s // 8, s % 8
    x, y, c = t // 8, (t // 2) % 4, t % 2

    def at(xh_, z_, x_, y_, c_):
        return (xh_ * 8 + z_, x_ * 8 + y_ * 2 + c_)

    sib = at(xh, z, x, y, 1 - c)
    xdev = at(xh, z, 1 - x, y, c)
    xhdev = at(1 - xh, z, x, y, c)
    zdev = (at(xh, (z + 1) % 8, x, y, c), at(xh, (z + 7) % 8, x, y, c))

    def ydev(o):
        return at(xh, z, x, (y + o) % 4, c)

    def remote(src, dst, ss, rs, dev):
        return pltpu.make_async_remote_copy(
            src_ref=src, dst_ref=dst, send_sem=ss, recv_sem=rs, device_id=dev, device_id_type=MESH
        )

    barrier = pltpu.get_barrier_semaphore()

    def greet(i, carry):
        pl.semaphore_signal(barrier, inc=1, device_id=(s, (t + i) % 16), device_id_type=MESH)
        return carry

    lax.fori_loop(1, 16, greet, 0)
    for dev in (xhdev,) + zdev:
        pl.semaphore_signal(barrier, inc=1, device_id=dev, device_id_type=MESH)

    def whole(ref, ss, rs):
        return remote(ref, ref, ss, rs, sib)

    def tokens(i):
        return (i % 8) // 4 * 8 + (i % 4) * 2 + i // 8

    def load_rows(src, dst, sem):
        def one(i, carry):
            row = pl.multiple_of(tokens(i) * 32, 32)
            pltpu.make_async_copy(src.at[pl.ds(row, 32)], dst.at[i], sem).start()
            return carry

        lax.fori_loop(0, 16, one, 0)

    def block_of(j, xo, co):
        dy = 2 - j + (j // 2) * (3 - 2 * (j % 2))
        return xo * 8 + (y + dy) % 4 * 2 + co

    def load_w(u):
        b = block_of(u // 2, (x + 1 + u % 2) % 2, 0) // 2
        col = pl.multiple_of(b * 1024, 1024)
        return pltpu.make_async_copy(weight.at[:, pl.ds(col, 1024)], w_v.at[u], sem_w.at[u])

    pltpu.make_async_copy(proj, pj.at[s], sem_proj).start()
    load_rows(attn, attn_v, sem_attn)
    for u in range(8):
        load_w(u).start()
    load_rows(resid, res_v, sem_res)
    pltpu.make_async_copy(student, stu_v, sem_stu).start()

    ring[:, 0, 0, 128:256] = jnp.zeros((2, 128, 512), BF16)
    ring[:, 1, 0, 0:128] = jnp.zeros((2, 128, 512), BF16)

    pl.semaphore_wait(barrier, 18)

    def cz(line, dr, j, p):
        sign = 1 - 2 * dr
        xx = xh if line == 1 else 1 - xh
        b = xx * 8 + (z - sign * (j - 1) + 8) % 8
        if j == 4:
            ref = pj.at[b, pl.ds(256 * dr + 128 * p, 128)]
        else:
            ref = pj.at[b, pl.ds(256 * p, 256)]
        return remote(ref, ref, cz_s, cz_r.at[line, dr, j - 1, p], zdev[dr])

    def cx():
        return remote(pj.at[s], pj.at[s], cx_s, cx_r, xhdev)

    def arrived(line, j, p):
        for dr in range(2):
            if j == 3:
                if p == 0:
                    cz(line, dr, j, 0).wait_recv()
                    cz(line, dr, j, 1).wait_recv()
            else:
                cz(line, dr, j, p).wait_recv()

    def forward(line, j, p):
        if j > 1:
            arrived(line, j - 1, p)
        for dr in range(2):
            cz(line, dr, j, p).start()

    pltpu.make_async_copy(proj, pj.at[s], sem_proj).wait()
    cx().start()
    forward(1, 1, 0)
    forward(1, 1, 1)

    def ac(j, xo):
        return remote(a_send.at[j, xo], a_crecv.at[j, xo], ac_s, ac_r.at[j, xo], sib)

    def ax(j):
        return remote(a_own.at[j, 1 - x, pl.ds(0, ROWS_A)], a_xrecv.at[j], ax_s, ax_r.at[j], xdev)

    def a_half(dr):
        return remote(
            a_own.at[0, x, pl.ds(HALF_A * dr, HALF_A)], ya_half.at[dr], ay_s.at[0], ay_r.at[0, dr], ydev(1 + 2 * dr)
        )

    def a_full(dr):
        return remote(
            a_own.at[1 + dr, x, pl.ds(0, ROWS_A)], ya_full.at[dr], ay_s.at[1], ay_r.at[1, dr], ydev(1 + 2 * dr)
        )

    def b_half(dr, xo):
        return remote(
            a_own.at[0, xo, pl.ds(ROWS_A + HALF_B * dr, HALF_B)], yb_half.at[dr, xo], by_s.at[0], by_r.at[0, dr, xo],
            ydev(1 + 2 * dr),
        )

    def b_full(dr, xo):
        return remote(
            a_own.at[1 + dr, xo, pl.ds(ROWS_A, 2 * HALF_B)], yb_full.at[dr, xo], by_s.at[1], by_r.at[1, dr, xo],
            ydev(1 + 2 * dr),
        )

    def bx():
        return remote(a_own.at[3, 1 - x, pl.ds(ROWS_A, 2 * HALF_B)], xb_recv, bx_s, bx_r, xdev)

    def product(u, co, out):
        j, xo = unit(u)
        cols = pl.ds(pl.multiple_of(co * 512, 512), 512)
        out[j, xo] = dot(attn_v[...].reshape(512, 512), w_v[u, :, cols]).astype(BF16)

    def unit(u):
        return u // 2, (x + 1 + u % 2) % 2

    def multiply(u):
        j, xo = unit(u)
        load_w(u).wait()
        product(u, 1 - c, a_send)
        ac(j, xo).start()
        product(u, c, a_own)

    def combine(u):
        j, xo = unit(u)
        ac(j, xo).wait_recv()
        a_own[j, xo] = (a_own[j, xo].astype(F32) + a_crecv[j, xo].astype(F32)).astype(BF16)

        @pl.when(u % 2 == 0)
        def _():
            ax(j).start()

        @pl.when(u < 2)
        def _():
            b_half(0, xo).start()
            b_half(1, xo).start()

    def send_b(dr, xo):
        rows = slice(ROWS_A + HALF_B * dr, ROWS_A + HALF_B * dr + HALF_B)
        b_half(dr, xo).wait_recv()
        a_own[1 + dr, xo, rows] = (a_own[1 + dr, xo, rows].astype(F32) + yb_half[dr, xo].astype(F32)).astype(BF16)
        b_full(dr, xo).start()

    def add_a(j):
        ax(j).wait_recv()
        a_own[j, x, 0:ROWS_A] = (a_own[j, x, 0:ROWS_A].astype(F32) + a_xrecv[j].astype(F32)).astype(BF16)

    pltpu.make_async_copy(attn, attn, sem_attn).wait()

    def teacher(u, carry):
        @pl.when(u < 8)
        def _():
            multiply(u)

        @pl.when(u >= 1)
        def _():
            combine(u - 1)

        @pl.when(u == 6)
        def _():
            forward(1, 2, 0)

        @pl.when(u == 7)
        def _():
            send_b(0, 1 - x)
            send_b(1, 1 - x)
            cx().wait_recv()
            forward(0, 1, 0)
            forward(0, 1, 1)

        return carry

    lax.fori_loop(0, 9, teacher, 0)

    def send_a(dr):
        rows = slice(HALF_A * dr, HALF_A * dr + HALF_A)
        add_a(1 + dr)
        a_half(dr).wait_recv()
        a_own[1 + dr, x, rows] = (a_own[1 + dr, x, rows].astype(F32) + ya_half[dr].astype(F32)).astype(BF16)
        a_full(dr).start()

    def sum_b(xo):
        b_full(0, xo).wait_recv()
        b_full(1, xo).wait_recv()
        a_own[3, xo, ROWS_A:512] = (
            a_own[3, xo, ROWS_A:512].astype(F32) + yb_full[0, xo].astype(F32) + yb_full[1, xo].astype(F32)
        ).astype(BF16)

    add_a(0)
    for dr in range(2):
        a_half(dr).start()
    for dr in range(2):
        send_b(dr, x)
    forward(0, 2, 0)
    forward(0, 2, 1)
    sum_b(1 - x)
    bx().start()
    forward(0, 3, 0)
    send_a(0)
    send_a(1)
    forward(0, 3, 1)
    add_a(3)
    forward(0, 4, 0)
    forward(0, 4, 1)
    forward(1, 2, 1)
    forward(1, 3, 0)
    sum_b(x)
    a_full(0).wait_recv()
    a_full(1).wait_recv()
    pltpu.make_async_copy(resid, resid, sem_res).wait()

    def finish(lo, hi, total):
        hidden = total + res_v[lo // 32 : hi // 32].astype(F32).reshape(hi - lo, 512)
        hg[lo:hi] = (hidden * gain[...].astype(F32).reshape(1, 512)).astype(BF16)
        sq = hidden * hidden
        sq = sq[:, 0:128] + sq[:, 128:256] + sq[:, 256:384] + sq[:, 384:512]
        pw[lo // 32 : hi // 32] = sq.reshape((hi - lo) // 32, 32, 128)

    finish(0, ROWS_A, a_own[3, x, 0:ROWS_A].astype(F32) + ya_full[0].astype(F32) + ya_full[1].astype(F32))
    bx().wait_recv()
    finish(ROWS_A, 512, a_own[3, x, ROWS_A:512].astype(F32) + xb_recv[...].astype(F32))

    def power(i):
        to = (t + i) % 16
        return remote(
            pw.at[to % 2 * 8 + to // 8 * 4 + to // 2 % 4], pw_recv.at[i], pw_s, pw_r, (s, to)
        )

    def send_power(i, carry):
        power(i).start()
        return carry

    lax.fori_loop(1, 16, send_power, 0)

    def root():
        whole(pw_recv.at[pl.ds(1, 15)], pw_s, pw_r).wait_recv()

        def one(i, total):
            return total + pw_recv[i]

        total = lax.fori_loop(1, 16, one, pw[c * 8 + x * 4 + y])
        mean = jnp.sum(total, axis=1, keepdims=True) * (1.0 / 8192)
        r_v[...] = jnp.broadcast_to(lax.rsqrt(mean + 1e-05), (32, 256))

    pltpu.make_async_copy(student, stu_v, sem_stu).wait()
    arrived(0, 4, 0)
    arrived(0, 4, 1)

    def block(q, m):
        line = (q + 3 + 2 * m) // 8
        off = (1 - 2 * m) * (4 - q - m + 4 * line)
        return (xh + 1 + line) % 2 * 8 + (z + off + 8) % 8

    def ds_(k, i):
        return d_s.at[k % 2, i], d_r.at[k % 8, i]

    def dc(k):
        return remote(t_send.at[k], t_crecv.at[k], *ds_(k, 0), sib)

    def dx(g, m):
        k = 2 * g + m
        if m == 0:
            return remote(t_own.at[k, 1 - x], xr0.at[g], *ds_(k, 1), xdev)
        return remote(t_own.at[k, 1 - x, y], xr1.at[g], *ds_(k, 1), xdev)

    def dy(g, m, o):
        k = 2 * g + m
        if m == 0:
            return remote(t_own.at[k, x, (y + o) % 4], yr0.at[g, o - 1], *ds_(k, 2), ydev(o))
        return remote(t_own.at[k, :, (y + o) % 4], yr1.at[g, o - 1], *ds_(k, 2), ydev(o))

    def ex(g, m):
        k = 2 * g + m
        ref = m_all.at[k, c, x] if m == 0 else m_all.at[k, c, x, y]
        return remote(ref, ref, *ds_(k, 3), xdev)

    def ey(g, m, o):
        k = 2 * g + m
        ref = m_all.at[k, c, x, y] if m == 0 else m_all.at[k, c, :, y]
        return remote(ref, ref, *ds_(k, 4), ydev(o))

    def y_arrived(g, m, i):
        whole(yr0.at[g] if m == 0 else yr1.at[g], *ds_(2 * g + m, i)).wait_recv()

    def ec(k):
        return remote(m_all.at[k, c], m_all.at[k, c], *ds_(k, 5), sib)

    def fz(line, dr, j, p, k):
        cols = pl.ds(256 * p, 256)
        return remote(
            g_send.at[k, :, cols], ring.at[line, dr, j, :, cols], f_s, f_r.at[line, dr, j, p],
            zdev[dr],
        )

    def fz_half(line, dr, p, k):
        rows, cols = pl.ds(128 * dr, 128), pl.ds(256 * p, 256)
        return remote(
            g_send.at[k, rows, cols], ring.at[line, dr, 0, rows, cols], f_s,
            f_r.at[line, dr, 0, p], zdev[dr],
        )

    def fx(p):
        cols = pl.ds(256 * p, 256)
        return remote(g_send.at[8, :, cols], rx.at[:, cols], fx_s, fx_r.at[p], xhdev)

    def core_rows(co):
        return pl.ds(pl.multiple_of(co * 256, 256), 256)

    def stage0(g, m):
        k = 2 * g + m
        b = block(g, m)
        t_send[k] = dot(hg[core_rows(1 - c)], pj[b]).astype(BF16).reshape(2, 4, 32, 256)
        dc(k).start()
        t_own[k] = dot(hg[core_rows(c)], pj[b]).astype(BF16).reshape(2, 4, 32, 256)

    def stage1(g, m):
        k = 2 * g + m
        dc(k).wait_recv()
        t_own[k] = (t_own[k].astype(F32) + t_crecv[k].astype(F32)).astype(BF16)
        if m == 0:
            dx(g, m).start()
        else:
            for o in (2, 1, 3):
                dy(g, m, o).start()

    def stage2(g, m):
        k = 2 * g + m
        if m == 0:
            dx(g, m).wait_recv()
            t_own[k, x] = (t_own[k, x].astype(F32) + xr0[g].astype(F32)).astype(BF16)
            for o in (2, 1, 3):
                dy(g, m, o).start()
        else:
            total = t_own[k, :, y].astype(F32)
            y_arrived(g, m, 2)
            for o in range(3):
                total = total + yr1[g, o].astype(F32)
            t_own[k, :, y] = total.astype(BF16)
            dx(g, m).start()

    def stage3(g, m):
        k = 2 * g + m
        if m == 0:
            total = t_own[k, x, y].astype(F32)
            y_arrived(g, m, 2)
            for o in range(3):
                total = total + yr0[g, o].astype(F32)
        else:
            dx(g, m).wait_recv()
            total = t_own[k, x, y].astype(F32) + xr1[g].astype(F32)
        cols = pl.ds(pl.multiple_of(block(g, m) * 256, 256), 256)
        mismatch = total * r_v[...] - stu_v[:, cols].astype(F32)
        mis_out[:, cols] = mismatch
        m_all[k, c, x, y] = (mismatch * r_v[...]).astype(BF16)
        if m == 0:
            for o in (2, 1, 3):
                ey(g, m, o).start()
        else:
            ex(g, m).start()

    def stage4(g, m):
        if m == 0:
            y_arrived(g, m, 4)
            ex(g, m).start()
        else:
            ex(g, m).wait_recv()
            for o in (2, 1, 3):
                ey(g, m, o).start()

    def stage5(g, m):
        if m == 0:
            ex(g, m).wait_recv()
        else:
            y_arrived(g, m, 4)
        ec(2 * g + m).start()

    def stage6(q, m):
        k = 2 * q + m
        ec(k).wait_recv()
        g_acc[m] = dot(m_all[k].reshape(512, 256), hg[...], ((0,), (0,)))
        reduce(q, m, 0)

    def stage7(q, m):
        reduce(q, m, 1)

    def reduce(q, m, p):
        k = 2 * q + m
        cols = slice(256 * p, 256 * p + 256)
        part = g_acc[m, :, cols]

        @pl.when(q == 3 * m)
        def _():
            g_send[k, :, cols] = part.astype(BF16)
            fz_half(m, 0, p, k).start()
            fz_half(m, 1, p, k).start()

        @pl.when(q == 4 + 3 * m)
        def _():
            for dr in range(2):
                fz(m, dr, 3, p, k).wait_recv()
            total = part + ring[m, 0, 3, :, cols].astype(F32) + ring[m, 1, 3, :, cols].astype(F32)
            if m == 0:
                g_send[k, :, cols] = total.astype(BF16)
                fx(p).start()
            else:
                fx(p).wait_recv()
                grad_out[:, cols] = (total + rx[:, cols].astype(F32)) * (1.0 / math.sqrt(8192))

        @pl.when((q != 3 * m) & (q != 4 + 3 * m))
        def _():
            line = (q + 3 + 2 * m) // 8
            j = q + m - 1 - 4 * line

            @pl.when(j == 0)
            def _():
                fz_half(line, m, p, k).wait_recv()

            @pl.when(j > 0)
            def _():
                fz(line, m, j, p, k).wait_recv()

            g_send[k, :, cols] = (part + ring[line, m, j, :, cols].astype(F32)).astype(BF16)
            fz(line, m, j + 1, p, k).start()

    stages = (stage0, stage1, stage2, stage3, stage4, stage5, stage6, stage7)

    def student_steps(h, carry):
        for par in range(2):
            for n in (0, 5, 4, 3, 2, 1, 7, 6):
                m = (par - STEPS[n]) % 2
                q = h + (par - STEPS[n] - m) // 2
                pl.when((q >= 0) & (q < BLOCKS))(lambda: stages[n](q, m))

            if par == 0:

                @pl.when(h == 1)
                def _():
                    forward(1, 3, 1)
                    root()

                @pl.when(h == 2)
                def _():
                    forward(1, 4, 0)
                    forward(1, 4, 1)

                @pl.when(h == 3)
                def _():
                    arrived(1, 4, 0)
                    arrived(1, 4, 1)

        return carry

    lax.fori_loop(0, BLOCKS + (STEPS[-1] + 1) // 2, student_steps, 0)

    for ref, sem in (
        (pj.at[s], cx_s), (pj.at[pl.ds(0, 14)], cz_s), (a_send, ac_s), (a_xrecv, ax_s), (ya_half, ay_s.at[0]),
        (ya_full, ay_s.at[1]), (yb_half, by_s.at[0]), (yb_full, by_s.at[1]), (xb_recv, bx_s),
        (pw_recv.at[pl.ds(1, 15)], pw_s), (g_send.at[pl.ds(0, 14)], f_s), (rx, fx_s),
        (t_send.at[pl.ds(0, 8)], d_s.at[0, 0]), (t_send.at[pl.ds(0, 8)], d_s.at[1, 0]),
        (xr0, d_s.at[0, 1]), (xr1, d_s.at[1, 1]), (yr0, d_s.at[0, 2]), (yr1, d_s.at[1, 2]),
        (xr0, d_s.at[0, 3]), (xr1, d_s.at[1, 3]), (yr0, d_s.at[0, 4]), (yr1, d_s.at[1, 4]),
        (t_send.at[pl.ds(0, 8)], d_s.at[0, 5]), (t_send.at[pl.ds(0, 8)], d_s.at[1, 5]),
    ):
        whole(ref, sem, pw_r).wait_send()


def shards(attn_heads, out_weight, residual, norm_gain, proj, student_hidden):
    hbm = pl.BlockSpec(memory_space=pl.ANY)
    vmem = pl.BlockSpec(memory_space=pltpu.VMEM)
    buf = lambda *shape: pltpu.VMEM(shape, BF16)
    dma = lambda *shape: pltpu.SemaphoreType.DMA(shape)
    return pl.pallas_call(
        kernel,
        name="distill",
        out_shape=(
            pltpu.VMEM((32, 4096), F32),
            pltpu.VMEM((256, 512), F32),
        ),
        in_specs=[hbm, hbm, hbm, vmem, hbm, hbm],
        out_specs=(vmem, vmem),
        scratch_shapes=[
            buf(16, 32, 512), buf(16, 32, 512), buf(8, 512, 1024), buf(32, 4096),
            buf(4, 2, 512, 512), buf(4, 2, 512, 512), buf(4, 2, 512, 512), buf(4, ROWS_A, 512),
            buf(2, HALF_A, 512), buf(2, ROWS_A, 512), buf(2, 2, HALF_B, 512), buf(2, 2, 2 * HALF_B, 512),
            buf(2 * HALF_B, 512),
            buf(512, 512), pltpu.VMEM((16, 32, 128), F32), pltpu.VMEM((16, 32, 128), F32),
            pltpu.VMEM((32, 256), F32),
            buf(16, 512, 256),
            buf(16, 2, 4, 32, 256), buf(16, 2, 4, 32, 256), buf(16, 2, 4, 32, 256),
            buf(8, 4, 32, 256), buf(8, 3, 32, 256), buf(8, 3, 2, 32, 256), buf(8, 32, 256),
            buf(16, 2, 2, 4, 32, 256),
            pltpu.VMEM((2, 256, 512), F32), buf(16, 256, 512), buf(2, 2, 4, 256, 512), buf(256, 512),
            dma(), dma(), dma(), dma(8), dma(),
            dma(), dma(4, 2), dma(), dma(4), dma(2), dma(2, 2), dma(2), dma(2, 2, 2), dma(), dma(),
            dma(), dma(), dma(), dma(), dma(), dma(2, 2, 4, 2),
            dma(2, 6), dma(8, 6), dma(), dma(2, 2, 4, 2), dma(), dma(2),
        ],
        compiler_params=pltpu.CompilerParams(
            collective_id=0, has_side_effects=True, vmem_limit_bytes=62 * 2**20
        ),
    )(attn_heads, out_weight, residual, norm_gain, proj, student_hidden)


def solution(mesh):
    return jax.shard_map(
        shards,
        mesh=mesh,
        in_specs=(
            P("seq", "tensor"),
            P("tensor", None),
            P("seq", "tensor"),
            P("tensor"),
            P("tensor", "seq"),
            P(("seq", "tensor"), None),
        ),
        out_specs=(P(("seq", "tensor"), None), P("seq", "tensor")),
        check_vma=False,
    )
```
